256 devices in a mesh: batch: 32 (over y, x, core), proto: 8 (over z).
Axes of the slice: x: 4, y: 4, z: 8, core: 2. Of those that a mesh axis runs over, the one named last changes fastest.
Arguments:
- student_feat: bfloat16 [5120, 256], P('batch'), may hold values from -30 to 30
- prototypes: bfloat16 [256, 131072], P('batch', 'proto'), may hold values from -480 to 480
- teacher_logits: float32 [1024, 131072], P('batch', 'proto'), may hold values from -1 to 1
Outputs:
- grad_feat: float32 [5120, 256], P('batch')
- grad_weight: float32 [256, 131072], P('batch', 'proto')
The draws below stay inside these ranges and needn't reach their ends.
All inputs are finite; a program needn't handle non-finite values.
Results may differ from the reference program's by a relative error of at most 0.0009.
Values may be sent and summed in bfloat16 or wider, within the bound.
No kernel may reach another device: no remote copies, remote signals or barrier semaphores. Data moves between devices by JAX's collectives and lax.ppermute only.
A program may use at most 128 MiB of HBM per device.

```python
import math
import jax
import jax.numpy as jnp
from jax import lax

D = 256
K = 131072
IMG_DEV = 16
CROPS = 10
GLOBAL = 2
ITERS = 3
ROWS = 5120
TEACH = 1024


def shared_direction(key):
    return jax.random.truncated_normal(key, -4.0, 4.0, (D,), jnp.float32) * 0.0625


def draw_prototypes(key, part):
    direction = shared_direction(key)
    key = jax.random.fold_in(key, 11)
    noise_key, load_key, column_key, row_key = jax.random.split(key, 4)
    noise_part = jax.random.truncated_normal(noise_key, -4.0, 4.0, (D, K), jnp.float32) * 0.0625
    loadings = jax.random.truncated_normal(load_key, -4.0, 4.0, (K,), jnp.float32) * 1.5
    column_scale = jnp.exp(jax.random.uniform(column_key, (K,), jnp.float32, 0.0, math.log(10.0)))
    row_ramp = jnp.power(3.0, jnp.arange(D, dtype=jnp.float32) / D)
    row_scale = row_ramp * jnp.exp(jax.random.uniform(row_key, (D,), jnp.float32, 0.0, math.log(4.0)))
    values = row_scale[:, None] * (noise_part + direction[:, None] * loadings[None, :]) * column_scale[None, :]
    return values.astype(jnp.bfloat16)


def draw_student_feat(key, part):
    direction = shared_direction(key)
    key = jax.random.fold_in(key, 23)
    noise_key, load_key, scale_key = jax.random.split(key, 3)
    noise_part = jax.random.truncated_normal(noise_key, -4.0, 4.0, (ROWS, D), jnp.float32) * 0.0625
    loadings = jax.random.truncated_normal(load_key, -4.0, 4.0, (ROWS,), jnp.float32) * 3.0
    row_scale = jnp.exp(jax.random.uniform(scale_key, (ROWS,), jnp.float32, 0.0, math.log(8.0)))
    values = row_scale[:, None] * (noise_part + loadings[:, None] * direction[None, :])
    return values.astype(jnp.bfloat16)


def draw_teacher_logits(key, part):
    key = jax.random.fold_in(key, 37)
    home_key, noise_key, gap_key, block_key, column_key, row_key, dead_key, level_key, slope_key = jax.random.split(key, 9)
    row_block = IMG_DEV * GLOBAL
    row_group = jnp.arange(TEACH, dtype=jnp.int32) // row_block % 4
    picked = jax.random.randint(home_key, (K,), 0, 10)
    home = jnp.where(picked < 4, 0, jnp.where(picked < 7, 1, jnp.where(picked < 9, 2, 3))).astype(jnp.int32)
    block_size = max(K // 8, 1)
    block_index = jnp.minimum(jnp.arange(K, dtype=jnp.int32) // block_size, 7)
    block_gap = jax.random.uniform(block_key, (8,), jnp.float32, 0.0, 1.0)[block_index]
    column_gap = 0.15 + 0.06 * block_gap + 0.06 * jax.random.uniform(gap_key, (K,), jnp.float32, 0.0, 1.0)
    noise_part = jax.random.uniform(noise_key, (TEACH, K), jnp.float32, -1.0, 1.0) * 0.12
    ramp_size = 0.044
    column_level = 0.15 * jax.random.uniform(column_key, (K,), jnp.float32, -1.0, 1.0)
    row_level = 0.1 * jax.random.uniform(row_key, (TEACH,), jnp.float32, -1.0, 1.0)
    row_sign = (2 * jax.random.randint(slope_key, (TEACH,), 0, 2) - 1).astype(jnp.float32)
    position = (jnp.arange(K, dtype=jnp.float32) + 0.5) / K * 2.0 - 1.0
    ramp = ramp_size * row_sign[:, None] * position[None, :]
    same = row_group[:, None] == home[None, :]
    values = 0.45 + noise_part + column_level[None, :] + row_level[:, None] + ramp - jnp.where(same, 0.0, column_gap[None, :])
    dead = jax.random.randint(dead_key, (TEACH, K), 0, 8) == 0
    dead_values = -1.0 + 0.4 * jax.random.uniform(level_key, (TEACH, K), jnp.float32, 0.0, 1.0)
    values = jnp.where(dead, dead_values, values)
    return values.astype(jnp.float32)


def setup_inputs(seed: int = 0) -> dict:
    key_list = jax.random.split(jax.random.key(seed), 4)
    student_feat = draw_student_feat(jax.random.fold_in(key_list[3], 71), 0)
    prototypes = draw_prototypes(jax.random.fold_in(key_list[3], 71), 0)
    teacher_logits = draw_teacher_logits(jax.random.fold_in(key_list[3], 71), 0)
    return dict(student_feat=student_feat, prototypes=prototypes, teacher_logits=teacher_logits)


STUDENT_TEMP = 0.1
TEACHER_TEMP = 0.04

def normalize_rows(student_feat):
    features = student_feat.astype(jnp.float32)
    feat_norm = jnp.sqrt(lax.optimization_barrier(jnp.sum(features * features, axis=1)) + 1e-06)
    unit_vec = features / feat_norm[:, None]
    return (feat_norm, unit_vec, unit_vec.astype(jnp.bfloat16))

def crop_targets(mass_block):
    images = mass_block.shape[0] // GLOBAL
    col_width = mass_block.shape[1]
    grouped = mass_block.reshape(images, GLOBAL, col_width)
    pair_sum = lax.optimization_barrier(jnp.sum(grouped, axis=1, keepdims=True))
    others = pair_sum - grouped
    distant = jnp.broadcast_to(pair_sum, (images, CROPS - GLOBAL, col_width))
    return jnp.concatenate([others, distant], axis=1).reshape(images * CROPS, col_width)

def pair_weights(row_count):
    crop_index = jnp.arange(row_count, dtype=jnp.int32) % CROPS
    return jnp.where(crop_index < GLOBAL, GLOBAL - 1, GLOBAL).astype(jnp.float32)

def reference(student_feat, prototypes, teacher_logits):
    feat_norm, unit_vec, unit_bf = normalize_rows(student_feat)
    weights_wide = prototypes.astype(jnp.float32)
    col_norm = jnp.sqrt(lax.optimization_barrier(jnp.sum(weights_wide * weights_wide, axis=0)) + 1e-06)
    col_scale = 1.0 / (col_norm * STUDENT_TEMP)
    teacher_mass = jnp.exp(teacher_logits / TEACHER_TEMP)
    for sweep_index in range(ITERS):
        teacher_mass = teacher_mass / lax.optimization_barrier(jnp.sum(teacher_mass, axis=0))[None, :]
        teacher_mass = teacher_mass / lax.optimization_barrier(jnp.sum(teacher_mass, axis=1))[:, None]
    row_count = unit_bf.shape[0]
    block_width = min(2048, K)
    block_count = K // block_width
    offsets = jnp.arange(block_count, dtype=jnp.int32) * block_width

    def first_pass(exp_total, offset):
        weight_block = lax.dynamic_slice_in_dim(prototypes, offset, block_width, 1)
        raw_scores = jnp.dot(unit_bf, weight_block, preferred_element_type=jnp.float32)
        scale_block = lax.dynamic_slice_in_dim(col_scale, offset, block_width, 0)
        logits = raw_scores * scale_block[None, :]
        return (exp_total + lax.optimization_barrier(jnp.sum(jnp.exp(logits), axis=1)), None)
    partition, unused = lax.scan(first_pass, jnp.zeros((row_count,), jnp.float32), offsets)
    pair_weight = pair_weights(row_count)
    pair_total = float(GLOBAL * CROPS - GLOBAL)

    def second_pass(unit_grad, offset):
        weight_block = lax.dynamic_slice_in_dim(prototypes, offset, block_width, 1)
        scale_block = lax.dynamic_slice_in_dim(col_scale, offset, block_width, 0)
        norm_block = lax.dynamic_slice_in_dim(col_norm, offset, block_width, 0)
        raw_scores = jnp.dot(unit_bf, weight_block, preferred_element_type=jnp.float32)
        logits = raw_scores * scale_block[None, :]
        prob = jnp.exp(logits) / partition[:, None]
        target = crop_targets(lax.dynamic_slice_in_dim(teacher_mass, offset, block_width, 1))
        grad_raw = ((pair_weight[:, None] * prob - target) / pair_total * scale_block[None, :]).astype(jnp.bfloat16)
        unit_grad = unit_grad + lax.dot_general(grad_raw, weight_block, (((1,), (1,)), ((), ())), preferred_element_type=jnp.float32)
        weight_term = lax.dot_general(unit_bf, grad_raw, (((0,), (0,)), ((), ())), preferred_element_type=jnp.float32)
        col_dot = lax.optimization_barrier(jnp.sum(grad_raw.astype(jnp.float32) * raw_scores, axis=0))
        grad_block = weight_term - weight_block.astype(jnp.float32) * (col_dot / (norm_block * norm_block))[None, :]
        return (unit_grad, grad_block)
    unit_grad, grad_blocks = lax.scan(second_pass, jnp.zeros((row_count, D), jnp.float32), offsets)
    grad_weight = jnp.moveaxis(grad_blocks, 0, 1).reshape(D, K)
    grad_feat = (unit_grad - unit_vec * lax.optimization_barrier(jnp.sum(unit_vec * unit_grad, axis=1, keepdims=True))) / feat_norm[:, None]
    return (grad_feat, grad_weight)
```

```python
import jax
import jax.numpy as jnp
from jax import lax
from jax.sharding import Mesh, PartitionSpec as P

CROPS = 10
GLOBAL = 2
STUDENT_TEMP = 0.1
TEACHER_TEMP = 0.04
PAIRS = float(GLOBAL * CROPS - GLOBAL)
F32 = jnp.float32
BF16 = jnp.bfloat16
PLANE = ("y", "x")
BATCH = ("y", "x", "core")
SWAP = ((0, 1), (1, 0))
SPAN = 250.0
LOW = 125.0
LOG2E = 1.4426950408889634


def normalize_rows(student_feat):
    features = student_feat.astype(F32)
    feat_norm = jnp.sqrt(jnp.sum(features * features, axis=1) + 1e-06)
    unit_vec = features / feat_norm[:, None]
    return (feat_norm, unit_vec, unit_vec.astype(BF16))


def encode_logits(x):
    mag = jnp.exp2(jnp.abs(x) * SPAN - LOW)
    return jnp.where(x < 0, -mag, mag).astype(BF16)


def decode_exp(code):
    v = code.astype(F32)
    mag = (jnp.log2(jnp.abs(v)) + LOW) * (LOG2E / (TEACHER_TEMP * SPAN))
    return jnp.exp2(jnp.where(v < 0, -mag, mag))


def root_code(x):
    y = x * x
    y = y * y
    y = y * y
    return jnp.where(x < 0, -y, y).astype(BF16)


def root_decode(code):
    v = code.astype(F32)
    y = jnp.sqrt(jnp.sqrt(jnp.sqrt(jnp.abs(v))))
    return jnp.where(v < 0, -y, y)


def split(x):
    hi = x.astype(BF16)
    return hi, (x - hi.astype(F32)).astype(BF16)


def dot(a, b, dims):
    return lax.dot_general(a, b, (dims, ((), ())), preferred_element_type=F32)


def shards(student_feat, prototypes, teacher_logits):
    core = lax.axis_index("core")
    feat_norm, unit_vec, unit_bf = normalize_rows(student_feat)

    tc = encode_logits(teacher_logits).reshape(32, 16, 2, 512).transpose(1, 2, 0, 3)
    tc = jnp.where(core == 0, tc, tc[:, ::-1]).reshape(16, 64, 512)
    wc = prototypes.reshape(8, 16, 2, 512).transpose(1, 2, 0, 3).reshape(16, 16, 512)
    st = unit_bf.reshape(2, 80, 256).transpose(1, 0, 2).reshape(1, 80, 512)
    send = jnp.concatenate([tc, wc, jnp.broadcast_to(st, (16, 80, 512))], axis=1)
    got = lax.all_to_all(send, PLANE, 0, 0, tiled=True)
    mate = lax.ppermute(got[:, 32:80], "core", SWAP)

    def by_core(own, other, axis):
        return jnp.stack([jnp.where(core == 0, own, other), jnp.where(core == 0, other, own)], axis=axis)

    mass = decode_exp(by_core(got[:, :32], mate[:, :32], 1).reshape(1024, 512))
    weights = by_core(got[:, 64:80].reshape(16, 2, 8, 512), mate[:, 32:48].reshape(16, 2, 8, 512), 1)
    weights = weights.transpose(0, 1, 3, 2, 4).reshape(256, 1024)
    units = got[:, 80:].reshape(16, 80, 2, 256).transpose(0, 2, 1, 3).reshape(2560, 256)

    wide = weights.astype(F32)
    norm_sq = jnp.sum(wide * wide, axis=0) + 1e-06
    col_scale = 1.0 / (jnp.sqrt(norm_sq) * STUDENT_TEMP)
    my_cols = core * 512
    my_weights = lax.dynamic_slice_in_dim(weights, my_cols, 512, 1)
    my_scale = lax.dynamic_slice_in_dim(col_scale, my_cols, 512, 0)
    my_norm_sq = lax.dynamic_slice_in_dim(norm_sq, my_cols, 512, 0)

    raw = dot(units, weights, ((1,), (0,)))
    prob = jnp.exp2(raw * (col_scale * LOG2E)[None, :])
    exp_part = jnp.sum(prob, axis=1)
    grad_prob = (prob * col_scale[None, :]).astype(BF16)

    grouped = units.reshape(256, CROPS, 256).astype(F32)
    total = jnp.sum(grouped, axis=1, keepdims=True)
    seen = (total - grouped[:, :GLOBAL]).reshape(16, 32, 256)
    seen = by_core(seen, lax.ppermute(seen, "core", SWAP), 1).reshape(1024, 256)

    col_inv = 1.0 / jnp.sum(mass, axis=0)
    row_part = jnp.sum(mass * col_inv[None, :], axis=1)
    pack = jnp.concatenate([row_part, exp_part]).reshape(1, 28, 128)
    came = lax.all_to_all(jnp.broadcast_to(pack, (32, 28, 128)), BATCH, 0, 0, tiled=True).reshape(16, 2, 28, 128)
    row_sum = jnp.sum(came[:, :, :8], axis=(0, 1))
    mine = jnp.where(core == 0, came[:, 0, 8:], came[:, 1, 8:])
    pack = jnp.concatenate([row_sum, jnp.sum(mine, axis=0)], axis=0)
    came = lax.all_to_all(jnp.broadcast_to(pack[None], (8, 28, 128)), "proto", 0, 0, tiled=True)
    came = jnp.sum(came, axis=0)
    row_inv = 1.0 / came[:8].reshape(1024)
    crop = jnp.arange(2560, dtype=jnp.int32) % CROPS
    weight = jnp.where(crop < GLOBAL, GLOBAL - 1, GLOBAL).astype(F32) / PAIRS
    factor = weight / came[8:].reshape(2560)

    col_inv = 1.0 / jnp.sum(mass * row_inv[:, None], axis=0)
    row_part = jnp.sum(mass * col_inv[None, :], axis=1).reshape(4, 256)
    row_part = row_part + lax.ppermute(row_part, "core", SWAP)
    student_part = dot(grad_prob, weights, ((1,), (1,))) * factor[:, None]
    hi, lo = split(row_part)
    rows = jnp.broadcast_to(jnp.concatenate([hi, lo])[None], (16, 8, 256))
    pad = jnp.zeros((16, 8, 256), BF16)
    pack = jnp.concatenate([root_code(student_part * 16384.0).reshape(16, 160, 256), rows, pad], axis=1)
    came = lax.all_to_all(pack, PLANE, 0, 0, tiled=True)
    home = jnp.sum(root_decode(came[:, :160]), axis=0) * (1.0 / 16384.0)
    row_sum = jnp.sum(came[:, 160:168].astype(F32), axis=0)
    row_sum = row_sum[:4] + row_sum[4:]
    pack = jnp.concatenate([home.reshape(8, 20, 256), jnp.broadcast_to(row_sum[None], (8, 4, 256))], axis=1)
    came = jnp.sum(lax.all_to_all(pack, "proto", 0, 0, tiled=True), axis=0)
    home_slice = came[:20]
    row_inv = 1.0 / came[20:].reshape(1024)

    scaled = units.astype(F32) * factor[:, None]
    hi, lo = split(scaled)
    term = dot(hi, grad_prob, ((0,), (0,))) + dot(lo, grad_prob, ((0,), (0,)))
    term = term.reshape(256, 2, 512)
    own = jnp.where(core == 0, term[:, 0], term[:, 1])
    other = jnp.where(core == 0, term[:, 1], term[:, 0])
    term = own + lax.ppermute(other, "core", SWAP)

    col_inv = 1.0 / jnp.sum(mass * row_inv[:, None], axis=0)
    row_part = jnp.sum(mass * col_inv[None, :], axis=1).reshape(4, 256)
    grad_target = (mass * (col_inv * my_scale)[None, :]).astype(BF16)
    target_part = dot(grad_target, my_weights, ((1,), (1,)))
    pack = jnp.concatenate(
        [target_part.reshape(32, 32, 256), jnp.broadcast_to(row_part[None], (32, 4, 256))], axis=1
    )
    came = jnp.sum(lax.all_to_all(pack, BATCH, 0, 0, tiled=True), axis=0)
    pack = jnp.concatenate([came, home_slice], axis=0)
    came = lax.all_to_all(jnp.broadcast_to(pack[None], (8, 56, 256)), "proto", 0, 0, tiled=True)
    student_home = came[:, 36:].reshape(160, 256)
    came = jnp.sum(came[:, :36], axis=0)
    row_inv = 1.0 / came[32:].reshape(1024)

    hi, lo = split(seen * (row_inv * (1.0 / PAIRS))[:, None])
    term = term - dot(hi, grad_target, ((0,), (0,))) - dot(lo, grad_target, ((0,), (0,)))
    my_wide = my_weights.astype(F32)
    col_dot = jnp.sum(my_wide * term, axis=0)
    grad = term - my_wide * (col_dot / my_norm_sq)[None, :]
    grad = lax.all_to_all(grad.reshape(32, 8, 512), BATCH, 0, 0, tiled=True)
    grad_weight = grad.transpose(1, 0, 2).reshape(8, 16384)

    index = lax.axis_index(BATCH)
    home_inv = lax.dynamic_slice_in_dim(row_inv, index * 32, 32, 0)
    target = (came[:32] * (home_inv * (1.0 / PAIRS))[:, None]).reshape(16, GLOBAL, 256)
    both = jnp.sum(target, axis=1, keepdims=True)
    rest = jnp.broadcast_to(both, (16, CROPS - GLOBAL, 256))
    target = jnp.concatenate([both - target, rest], axis=1).reshape(160, 256)
    unit_total = student_home - target
    grad_feat = (unit_total - unit_vec * jnp.sum(unit_vec * unit_total, axis=1, keepdims=True)) / feat_norm[:, None]
    return (grad_feat, grad_weight)


def solution(mesh):
    split_mesh = Mesh(mesh.devices.reshape(4, 4, 2, 8), ("y", "x", "core", "proto"))
    return jax.shard_map(
        shards,
        mesh=split_mesh,
        in_specs=(P(BATCH, None), P(BATCH, "proto"), P(BATCH, "proto")),
        out_specs=(P(BATCH, None), P(BATCH, "proto")),
        check_vma=False,
    )
```

```python
import jax
import jax.numpy as jnp
from jax import lax
from jax.sharding import Mesh, PartitionSpec as P

CROPS = 10
GLOBAL = 2
STUDENT_TEMP = 0.1
TEACHER_TEMP = 0.04
PAIRS = float(GLOBAL * CROPS - GLOBAL)
F32 = jnp.float32
BF16 = jnp.bfloat16
PLANE = ("y", "x")
BATCH = ("y", "x", "core")
SWAP = ((0, 1), (1, 0))
SPAN = 250.0
LOW = 125.0
LOG2E = 1.4426950408889634
ROOT = 3276.8


def normalize_rows(student_feat):
    features = student_feat.astype(F32)
    feat_norm = jnp.sqrt(jnp.sum(features * features, axis=1) + 1e-06)
    unit_vec = features / feat_norm[:, None]
    return (feat_norm, unit_vec, unit_vec.astype(BF16))


def encode_logits(x):
    mag = jnp.exp2(jnp.abs(x) * SPAN - LOW)
    return jnp.where(x < 0, -mag, mag).astype(BF16)


def decode_exp(code):
    v = code.astype(F32)
    mag = (jnp.log2(jnp.abs(v)) + LOW) * (LOG2E / (TEACHER_TEMP * SPAN))
    return jnp.exp2(jnp.where(v < 0, -mag, mag))


def root_code(x):
    y = x * x
    y = y * y
    y = y * y
    return jnp.where(x < 0, -y, y).astype(BF16)


def root_decode(code):
    v = code.astype(F32)
    y = jnp.sqrt(jnp.sqrt(jnp.sqrt(jnp.abs(v))))
    return jnp.where(v < 0, -y, y)


def split(x):
    hi = x.astype(BF16)
    return hi, (x - hi.astype(F32)).astype(BF16)


def dot(a, b, dims):
    return lax.dot_general(a, b, (dims, ((), ())), preferred_element_type=F32)


def shards(student_feat, prototypes, teacher_logits):
    core = lax.axis_index("core")
    feat_norm, unit_vec, unit_bf = normalize_rows(student_feat)

    tc = encode_logits(teacher_logits).reshape(32, 16, 2, 512).transpose(1, 2, 0, 3)
    tc = jnp.where(core == 0, tc, tc[:, ::-1]).reshape(16, 64, 512)
    wc = prototypes.reshape(8, 16, 2, 512).transpose(1, 2, 0, 3).reshape(16, 16, 512)
    st = unit_bf.reshape(2, 80, 256).transpose(1, 0, 2).reshape(1, 80, 512)
    send = jnp.concatenate([tc, wc, jnp.broadcast_to(st, (16, 80, 512))], axis=1)
    got = lax.all_to_all(send, PLANE, 0, 0, tiled=True)
    mate = lax.ppermute(got[:, 32:80], "core", SWAP)

    def by_core(own, other, axis):
        return jnp.stack([jnp.where(core == 0, own, other), jnp.where(core == 0, other, own)], axis=axis)

    mass = decode_exp(by_core(got[:, :32], mate[:, :32], 1).reshape(1024, 512))
    weights = by_core(got[:, 64:80].reshape(16, 2, 8, 512), mate[:, 32:48].reshape(16, 2, 8, 512), 1)
    weights = weights.transpose(0, 1, 3, 2, 4).reshape(256, 1024)
    units = got[:, 80:].reshape(16, 80, 2, 256).transpose(0, 2, 1, 3).reshape(2560, 256)

    wide = weights.astype(F32)
    norm_sq = jnp.sum(wide * wide, axis=0) + 1e-06
    col_scale = 1.0 / (jnp.sqrt(norm_sq) * STUDENT_TEMP)
    my_cols = core * 512
    my_weights = lax.dynamic_slice_in_dim(weights, my_cols, 512, 1)
    my_scale = lax.dynamic_slice_in_dim(col_scale, my_cols, 512, 0)
    my_norm_sq = lax.dynamic_slice_in_dim(norm_sq, my_cols, 512, 0)

    col_inv = 1.0 / jnp.sum(mass, axis=0)
    row_part = jnp.sum(mass * col_inv[None, :], axis=1)
    came = lax.all_to_all(jnp.broadcast_to(row_part.reshape(1, 8, 128), (32, 8, 128)), BATCH, 0, 0, tiled=True)
    row_sum = jnp.sum(came, axis=0)
    came = lax.all_to_all(jnp.broadcast_to(row_sum[None], (8, 8, 128)), "proto", 0, 0, tiled=True)
    row_inv = 1.0 / jnp.sum(came, axis=0).reshape(1024)

    raw = dot(units, weights, ((1,), (0,)))
    prob = jnp.exp2(raw * (col_scale * LOG2E)[None, :])
    exp_part = jnp.sum(prob, axis=1)
    grad_prob = (prob * col_scale[None, :]).astype(BF16)
    student_code = root_code(dot(grad_prob, weights, ((1,), (1,))) * (ROOT / exp_part)[:, None])
    exp_hi, exp_lo = split(exp_part.reshape(10, 256))

    grouped = units.reshape(256, CROPS, 256).astype(F32)
    total = jnp.sum(grouped, axis=1, keepdims=True)
    seen = (total - grouped[:, :GLOBAL]).reshape(16, 32, 256)
    seen = by_core(seen, lax.ppermute(seen, "core", SWAP), 1).reshape(1024, 256)

    col_inv = 1.0 / jnp.sum(mass * row_inv[:, None], axis=0)
    row_part = jnp.sum(mass * col_inv[None, :], axis=1).reshape(4, 256)
    row_part = row_part + lax.ppermute(row_part, "core", SWAP)
    hi, lo = split(row_part)
    rows = jnp.concatenate([exp_hi, exp_lo, hi, lo, jnp.zeros((4, 256), BF16)], axis=0)
    pack = jnp.concatenate([student_code.reshape(16, 160, 256), jnp.broadcast_to(rows[None], (16, 32, 256))], axis=1)
    came = lax.all_to_all(pack, PLANE, 0, 0, tiled=True)
    student_came = came[:, :160]
    extra = came[:, 160:].astype(F32)
    exp_came = (extra[:, :10] + extra[:, 10:20]).reshape(16, 2560)
    row_sum = jnp.sum(extra[:, 20:24] + extra[:, 24:28], axis=0).reshape(8, 128)
    exp_sum = jnp.sum(exp_came, axis=0).reshape(20, 128)
    place = lax.axis_index(PLANE) * 160
    parts = lax.dynamic_slice_in_dim(exp_came, place, 160, 1) * (1.0 / ROOT)
    home = jnp.sum(root_decode(student_came) * parts[:, :, None], axis=0)
    pack = jnp.concatenate([row_sum, exp_sum], axis=0)
    pack = jnp.concatenate(
        [jnp.broadcast_to(pack.reshape(1, 14, 256), (8, 14, 256)), home.reshape(8, 20, 256)], axis=1
    )
    came = jnp.sum(lax.all_to_all(pack, "proto", 0, 0, tiled=True), axis=0)
    row_inv = 1.0 / came[:4].reshape(1024)
    crop = jnp.arange(2560, dtype=jnp.int32) % CROPS
    weight = jnp.where(crop < GLOBAL, GLOBAL - 1, GLOBAL).astype(F32) / PAIRS
    factor = weight / came[4:14].reshape(2560)
    home_slice = came[14:]

    scaled = units.astype(F32) * factor[:, None]
    hi, lo = split(scaled)
    term = dot(hi, grad_prob, ((0,), (0,))) + dot(lo, grad_prob, ((0,), (0,)))
    term = term.reshape(256, 2, 512)
    own = jnp.where(core == 0, term[:, 0], term[:, 1])
    other = jnp.where(core == 0, term[:, 1], term[:, 0])
    term = own + lax.ppermute(other, "core", SWAP)

    index = lax.axis_index(BATCH)
    col_inv = 1.0 / jnp.sum(mass * row_inv[:, None], axis=0)
    row_part = jnp.sum(mass * col_inv[None, :], axis=1)
    grad_target = (mass * (col_inv * my_scale)[None, :]).astype(BF16)
    target_code = root_code(dot(grad_target, my_weights, ((1,), (1,))) * (ROOT / row_part)[:, None])
    hi, lo = split(row_part.reshape(4, 256))
    rows = jnp.concatenate([hi, lo, jnp.zeros((8, 256), BF16)], axis=0)
    pack = jnp.concatenate([target_code.reshape(32, 32, 256), jnp.broadcast_to(rows[None], (32, 16, 256))], axis=1)
    came = lax.all_to_all(pack, BATCH, 0, 0, tiled=True)
    extra = came[:, 32:].astype(F32)
    row_came = (extra[:, :4] + extra[:, 4:8]).reshape(32, 1024)
    parts = lax.dynamic_slice_in_dim(row_came, index * 32, 32, 1) * (1.0 / ROOT)
    target = jnp.sum(root_decode(came[:, :32]) * parts[:, :, None], axis=0)
    row_sum = jnp.sum(row_came, axis=0).reshape(4, 256)
    pack = jnp.concatenate([row_sum, target, home_slice], axis=0)
    came = lax.all_to_all(jnp.broadcast_to(pack[None], (8, 56, 256)), "proto", 0, 0, tiled=True)
    home_factor = lax.dynamic_slice_in_dim(factor, place, 160, 0)
    student_home = came[:, 36:].reshape(160, 256) * home_factor[:, None]
    came = jnp.sum(came[:, :36], axis=0)
    row_inv = 1.0 / came[:4].reshape(1024)

    hi, lo = split(seen * (row_inv * (1.0 / PAIRS))[:, None])
    term = term - dot(hi, grad_target, ((0,), (0,))) - dot(lo, grad_target, ((0,), (0,)))
    my_wide = my_weights.astype(F32)
    col_dot = jnp.sum(my_wide * term, axis=0)
    grad = term - my_wide * (col_dot / my_norm_sq)[None, :]
    grad = lax.all_to_all(grad.reshape(32, 8, 512), BATCH, 0, 0, tiled=True)
    grad_weight = grad.transpose(1, 0, 2).reshape(8, 16384)

    home_inv = lax.dynamic_slice_in_dim(row_inv, index * 32, 32, 0)
    target = (came[4:] * (home_inv * (1.0 / PAIRS))[:, None]).reshape(16, GLOBAL, 256)
    both = jnp.sum(target, axis=1, keepdims=True)
    rest = jnp.broadcast_to(both, (16, CROPS - GLOBAL, 256))
    target = jnp.concatenate([both - target, rest], axis=1).reshape(160, 256)
    unit_total = student_home - target
    grad_feat = (unit_total - unit_vec * jnp.sum(unit_vec * unit_total, axis=1, keepdims=True)) / feat_norm[:, None]
    return (grad_feat, grad_weight)


def solution(mesh):
    split_mesh = Mesh(mesh.devices.reshape(4, 4, 2, 8), ("y", "x", "core", "proto"))
    return jax.shard_map(
        shards,
        mesh=split_mesh,
        in_specs=(P(BATCH, None), P(BATCH, "proto"), P(BATCH, "proto")),
        out_specs=(P(BATCH, None), P(BATCH, "proto")),
        check_vma=False,
    )
```

```python
import jax
import jax.numpy as jnp
from jax import lax
from jax.experimental import pallas as pl
from jax.experimental.pallas import tpu as pltpu
from jax.sharding import Mesh, PartitionSpec as P

CROPS = 10
GLOBAL = 2
STUDENT_TEMP = 0.1
TEACHER_TEMP = 0.04
PAIRS = float(GLOBAL * CROPS - GLOBAL)
F32 = jnp.float32
BF16 = jnp.bfloat16
PLANE = ("y", "x")
BATCH = ("y", "x", "core")
SWAP = ((0, 1), (1, 0))
SPAN = 250.0
LOW = 125.0
LOG2E = 1.4426950408889634
ROOT = 3276.8
WIDE = 16384.0
TINY = 1e-38


def encode_logits(x):
    mag = jnp.exp2(jnp.abs(x) * SPAN - LOW)
    return jnp.where(x < 0, -mag, mag).astype(BF16)


def decode_exp(code):
    v = code.astype(F32)
    mag = (jnp.log2(jnp.abs(v)) + LOW) * (LOG2E / (TEACHER_TEMP * SPAN))
    return jnp.exp2(jnp.where(v < 0, -mag, mag))


def root_code(x):
    y = x * x
    y = y * y
    return jnp.where(x < 0, -y, y)


def root_decode(code):
    v = code.astype(F32)
    y = lax.rsqrt(lax.rsqrt(jnp.abs(v) + TINY))
    return jnp.where(v < 0, -y, y)


def fine_code(x):
    y = x * x
    y = y * y
    y = y * y
    return jnp.where(x < 0, -y, y)


def fine_decode(code):
    v = code.astype(F32)
    y = jnp.sqrt(lax.rsqrt(lax.rsqrt(jnp.abs(v) + TINY)))
    return jnp.where(v < 0, -y, y)


def sum_code(x):
    y = x * (1.0 / 1024.0)
    y = y * y
    y = y * y
    return y * y


def sum_decode(code):
    return jnp.sqrt(lax.rsqrt(lax.rsqrt(code.astype(F32)))) * 1024.0


def split(x):
    hi = x.astype(BF16)
    return hi, (x - hi.astype(F32)).astype(BF16)


def dot(a, b, dims):
    return lax.dot_general(a, b, (dims, ((), ())), preferred_element_type=F32)


NN = ((1,), (0,))
NT = ((1,), (1,))
TN = ((0,), (0,))


def lanes(x8):
    return jnp.concatenate([x8[i : i + 1] for i in range(8)], axis=1)


def rows8(x):
    return jnp.concatenate([x[:, 128 * i : 128 * (i + 1)] for i in range(8)], axis=0)


def split_row(x8):
    hi = x8.astype(BF16).astype(F32)
    return jnp.concatenate([hi, x8 - hi], axis=1)


def join_row(x):
    return x[:, :128] + x[:, 128:]


def padded(x8):
    return jnp.concatenate([x8, jnp.zeros_like(x8)], axis=0).astype(BF16)


def sweep(mass_ref, row_inv, keep_ref=None, copies=None):
    total = jnp.zeros((8, 1024), F32)
    for low in range(0, 512, 32):
        if copies is not None and low % 128 == 0:
            copies[low // 128].wait()
        x = mass_ref[low : low + 32, :]
        y = x if row_inv is None else x * row_inv
        x = x * (1.0 / jnp.sum(y, axis=1, keepdims=True))
        if keep_ref is not None:
            keep_ref[low : low + 32, :] = x.astype(BF16)
        total = total + ((x[:8] + x[8:16]) + (x[16:24] + x[24:]))
    return jnp.sum(total, axis=0, keepdims=True)


def pack_kernel(core_ref, teacher_ref, proto_ref, feat_ref, out_ref, unit_ref):
    first = core_ref[0] == 0

    @pl.when(pl.program_id(0) == 0)
    def _():
        x = feat_ref[...].astype(F32)
        unit = x / jnp.sqrt(jnp.sum(x * x, axis=1, keepdims=True) + 1e-06)
        unit = unit.astype(BF16)
        unit_ref[:, :256] = unit[:80]
        unit_ref[:, 256:] = unit[80:]

    for p in range(4):
        left = encode_logits(teacher_ref[:, 1024 * p : 1024 * p + 512])
        right = encode_logits(teacher_ref[:, 1024 * p + 512 : 1024 * p + 1024])
        out_ref[p, 0:32, :] = jnp.where(first, left, right)
        out_ref[p, 32:64, :] = jnp.where(first, right, left)
        w = proto_ref[:, 1024 * p : 1024 * p + 1024].astype(F32)
        out_ref[p, 64:80, :] = jnp.concatenate([w[:, :512], w[:, 512:]], axis=0).astype(BF16)
        out_ref[p, 80:160, :] = unit_ref[...]


def first_kernel(core_ref, own_ref, mate_ref, mass_ref, out_ref):
    first = core_ref[0] == 0
    for j in range(4):
        own = decode_exp(own_ref[4 * j : 4 * j + 4].reshape(128, 512)).T
        mate = decode_exp(mate_ref[4 * j : 4 * j + 4].reshape(128, 512)).T
        mass_ref[:, 128 * j : 128 * j + 128] = jnp.where(first, own, mate)
        mass_ref[:, 512 + 128 * j : 640 + 128 * j] = jnp.where(first, mate, own)
    part = rows8(sweep(mass_ref, None))
    out_ref[...] = jnp.broadcast_to(part[None], (32, 8, 128))


def fetch(mass_hbm, mass_ref, sems):
    copies = [
        pltpu.make_async_copy(
            mass_hbm.at[pl.ds(128 * i, 128), :], mass_ref.at[pl.ds(128 * i, 128), :], sems.at[i]
        )
        for i in range(4)
    ]
    for copy in copies:
        copy.start()
    return copies


def second_kernel(came_ref, mass_hbm, out_ref, mass_ref, sems):
    copies = fetch(mass_hbm, mass_ref, sems)
    row_inv = lanes(1.0 / jnp.sum(came_ref[...], axis=0))
    out_ref[...] = rows8(sweep(mass_ref, row_inv, copies=copies))


def insert_kernel(own_ref, mate_ref, pack_ref, out_ref):
    row = padded(split_row(own_ref[...] + mate_ref[...]))
    out_ref[...] = jnp.broadcast_to(row[None], (16, 16, 256))


def home_kernel(place_ref, came_ref, out_ref, home_ref, exp_ref, row_ref, part_ref):
    step = pl.program_id(0)

    @pl.when(step == 0)
    def _():
        home_ref[...] = jnp.zeros_like(home_ref)
        exp_ref[...] = jnp.zeros_like(exp_ref)
        row_ref[...] = jnp.zeros_like(row_ref)
        part_ref[...] = jnp.zeros_like(part_ref)

    pick = lax.broadcasted_iota(jnp.int32, (16, 256), 0) == place_ref[0]
    exp_sum = exp_ref[...]
    row_sum = row_ref[...]
    parts = []
    for p in range(4):
        exp_part = sum_decode(came_ref[p, 160:176, :])
        exp_sum = exp_sum + exp_part
        row_sum = row_sum + came_ref[p, 176:192, :].astype(F32)[:8]
        parts.append(jnp.sum(jnp.where(pick, exp_part, 0.0), axis=0, keepdims=True))
    exp_ref[...] = exp_sum
    row_ref[...] = row_sum
    parts = columns(jnp.concatenate(parts + [jnp.zeros((4, 256), F32)], axis=0) * (1.0 / ROOT))
    part_ref[...] += jnp.sum(parts, axis=1, keepdims=True)
    for low in range(0, 160, 32):
        home = home_ref[low : low + 32, :]
        for p in range(4):
            home = home + root_decode(came_ref[p, low : low + 32, :]) * parts[low : low + 32, p : p + 1]
        home_ref[low : low + 32, :] = home

    @pl.when(step == 3)
    def _():
        code = fine_code(home_ref[...] / part_ref[:160, :1])
        tail = [jnp.zeros((4, 256), F32), split_row(join_row(row_ref[...])), sum_code(exp_ref[...] * (1.0 / 16.0))]
        for z in range(8):
            out_ref[z] = jnp.concatenate([code[20 * z : 20 * z + 20]] + tail, axis=0).astype(BF16)


def slice_kernel(place_ref, came_ref, out_ref):
    pick = lax.broadcasted_iota(jnp.int32, (16, 256), 0) == place_ref[0]
    parts = []
    for p in range(8):
        exp_part = sum_decode(came_ref[p, 32:48, :]) * 16.0
        parts.append(jnp.sum(jnp.where(pick, exp_part, 0.0), axis=0, keepdims=True))
    parts = pltpu.roll(jnp.concatenate(parts, axis=0), (256 - 20 * place_ref[1]) % 256, 1)
    parts = columns(parts)[:32]
    home = jnp.zeros((32, 256), F32)
    for p in range(8):
        home = home + fine_decode(came_ref[p, 0:32, :]) * parts[:, p : p + 1]
    row = lax.broadcasted_iota(jnp.int32, (32, 1), 0)
    weight = jnp.where(row % CROPS < GLOBAL, (GLOBAL - 1) / PAIRS, GLOBAL / PAIRS) * (WIDE / ROOT)
    out_ref[...] = fine_code(home * (weight / jnp.sum(parts, axis=1, keepdims=True)))[:24]


def third_kernel(came_ref, mass_ref, hi_ref, lo_ref, keep_ref, out_ref):
    rows = came_ref[0, 16:32, :].astype(F32)
    for p in range(1, 8):
        rows = rows + came_ref[p, 16:32, :].astype(F32)
    row_inv = lanes(1.0 / join_row(rows[8:]))
    part = sweep(mass_ref, row_inv, keep_ref)
    scale = ROOT / part
    for j in range(8):
        keep = keep_ref[:, 128 * j : 128 * j + 128]
        x = jnp.dot(hi_ref[...], keep, preferred_element_type=F32)
        x = x + jnp.dot(lo_ref[...], keep, preferred_element_type=F32)
        x = (x * scale[:, 128 * j : 128 * j + 128]).T
        x = root_code(x).astype(BF16)
        for i in range(4):
            block = 4 * j + i
            out_ref[block % 16 * 2 + block // 16, 0:32, :] = x[32 * i : 32 * i + 32]
    out_ref[:, 32:48, :] = jnp.broadcast_to(padded(split_row(rows8(part)))[None], (32, 16, 256))


def target_kernel(index_ref, came_ref, slice_ref, out_ref, turn_ref):
    index = index_ref[0]
    pick = lax.broadcasted_iota(jnp.int32, (8, 128), 0) == index // 4
    row_sum = jnp.zeros((8, 128), F32)
    parts = []
    for p in range(32):
        row = join_row(came_ref[p, 32:48, :].astype(F32)[:8])
        row_sum = row_sum + row
        parts.append(jnp.sum(jnp.where(pick, row, 0.0), axis=0, keepdims=True))
    parts = jnp.concatenate(parts, axis=0) * (1.0 / ROOT)
    turn_ref[...] = jnp.concatenate([parts, jnp.zeros((96, 128), F32)], axis=0).T
    parts = turn_ref[pl.ds(pl.multiple_of(index % 4 * 32, 32), 32), :]
    total = jnp.zeros((32, 256), F32)
    for p in range(32):
        total = total + root_decode(came_ref[p, 0:32, :]) * parts[:, p : p + 1]
    code = fine_code(total / jnp.sum(parts, axis=1, keepdims=True))
    code = jnp.concatenate([code, slice_ref[...], split_row(row_sum)], axis=0).astype(BF16)
    out_ref[...] = jnp.broadcast_to(code[None], (8, 64, 256))


def feat_kernel(index_ref, came_ref, feat_ref, out_ref, turn_ref):
    index = index_ref[0]
    pick = lax.broadcasted_iota(jnp.int32, (8, 128), 0) == index // 4
    parts = []
    for p in range(8):
        row = join_row(came_ref[p, 48:64, :].astype(F32)[8:])
        parts.append(jnp.sum(jnp.where(pick, row, 0.0), axis=0, keepdims=True))
    parts = jnp.concatenate(parts + [jnp.zeros((120, 128), F32)], axis=0)
    turn_ref[...] = parts.T
    parts = turn_ref[pl.ds(pl.multiple_of(index % 4 * 32, 32), 32), :]
    target = jnp.zeros((32, 256), F32)
    for p in range(8):
        target = target + fine_decode(came_ref[p, 0:32, :]) * parts[:, p : p + 1]
    target = target / jnp.sum(parts, axis=1, keepdims=True) * (1.0 / (ROOT * PAIRS))
    hi, lo = split(target)
    row = lax.broadcasted_iota(jnp.int32, (160, 32), 0)
    col = lax.broadcasted_iota(jnp.int32, (160, 32), 1)
    keep = jnp.where((row // CROPS == col // GLOBAL) & (row % CROPS != col % GLOBAL), 1.0, 0.0).astype(BF16)
    student = [fine_decode(came_ref[p, 32:64, :])[:20] for p in range(8)]
    total = jnp.concatenate(student, axis=0) * (1.0 / WIDE) - (dot(keep, hi, NN) + dot(keep, lo, NN))
    x = feat_ref[...].astype(F32)
    norm = jnp.sqrt(jnp.sum(x * x, axis=1, keepdims=True) + 1e-06)
    unit = x / norm
    out_ref[...] = (total - unit * jnp.sum(unit * total, axis=1, keepdims=True)) / norm


def final_kernel(
    core_ref, came_ref, keep_ref, seen_ref, mate_ref, term_ref, term_mate_ref, weight_ref, scale_ref, inv_ref, out_ref,
    hi_ref, lo_ref,
):
    @pl.when(pl.program_id(0) == 0)
    def _():
        first = core_ref[0] == 0
        rows = came_ref[0, 48:64, :].astype(F32)
        for p in range(1, 8):
            rows = rows + came_ref[p, 48:64, :].astype(F32)
        row_inv = lanes(1.0 / join_row(rows[8:])) * (1.0 / PAIRS)
        seen = seen_ref[...]
        mate = mate_ref[...]
        hi_ref[:, :512], lo_ref[:, :512] = split(jnp.where(first, seen, mate) * row_inv[:, :512])
        hi_ref[:, 512:], lo_ref[:, 512:] = split(jnp.where(first, mate, seen) * row_inv[:, 512:])

    keep = keep_ref[...]
    x = dot(hi_ref[...], keep, NT) + dot(lo_ref[...], keep, NT)
    x = term_ref[...] + term_mate_ref[...] - x * scale_ref[...]
    w = weight_ref[...].astype(F32)
    dots = jnp.sum(w * x, axis=0, keepdims=True) * inv_ref[...]
    out_ref[...] = x - w * dots


def columns(x):
    return jnp.concatenate([x, jnp.zeros((120, 256), F32)], axis=0).T


def exp_kernel(
    core_ref, own_ref, mate_ref, unit_ref, out_ref, sum_ref, all_ref, my_ref, my_scale_ref, my_inv_ref, hi_ref, lo_ref,
    scale_ref,
):
    step = pl.program_id(0)

    @pl.when(step == 0)
    def _():
        first = core_ref[0] == 0
        squares = jnp.zeros((8, 1024), F32)
        for p in range(16):
            own = own_ref[p].astype(F32)
            mate = mate_ref[p].astype(F32)
            low = jnp.where(first, own, mate)
            high = jnp.where(first, mate, own)
            left = jnp.concatenate([low[:8], high[:8]], axis=0)
            right = jnp.concatenate([low[8:], high[8:]], axis=0)
            rows = slice(16 * p, 16 * p + 16)
            all_ref[rows, :512] = left.astype(BF16)
            all_ref[rows, 512:] = right.astype(BF16)
            my_ref[rows, :] = jnp.where(first, left, right).astype(BF16)
            both = jnp.concatenate([left, right], axis=1)
            both = both * both
            squares = squares + (both[:8] + both[8:])
        norm_sq = jnp.sum(squares, axis=0, keepdims=True) + 1e-06
        scale = 1.0 / (jnp.sqrt(norm_sq) * STUDENT_TEMP)
        scale_ref[...] = scale
        my_inv_ref[...] = 1.0 / jnp.where(first, norm_sq[:, :512], norm_sq[:, 512:])
        my_scale = jnp.where(first, scale[:, :512], scale[:, 512:])
        my_scale_ref[...] = my_scale
        for p in range(8):
            rows = slice(32 * p, 32 * p + 32)
            hi, lo = split(my_ref[rows, :].astype(F32) * my_scale)
            hi_ref[rows, :] = hi
            lo_ref[rows, :] = lo

    scale = scale_ref[...]
    power = scale * LOG2E
    sums = []
    for p in range(4):
        for half in range(2):
            raw = dot(unit_ref[p, :, 256 * half : 256 * half + 256], all_ref[...], NN)
            prob = jnp.exp2(raw * power)
            sums.append(jnp.sum(prob, axis=1, keepdims=True))
            out_ref[160 * p + 80 * half : 160 * p + 80 * half + 80, :] = (prob * scale).astype(BF16)
    sums = [jnp.concatenate(sums[2 * p : 2 * p + 2], axis=0) for p in range(4)]
    sums = jnp.concatenate(sums + [jnp.ones((160, 124), F32)], axis=1)
    sums = jnp.concatenate([sums, jnp.ones((96, 128), F32)], axis=0).T[:4]
    row = lax.broadcasted_iota(jnp.int32, (16, 256), 0)
    sum_ref[...] = jnp.where(row // 4 == step, jnp.concatenate([sums] * 4, axis=0), sum_ref[...])


def student_kernel(grad_ref, weight_ref, part_ref, sum_ref, out_ref):
    scale = columns(ROOT / part_ref[...])
    sums = sum_code(sum_ref[...]).astype(BF16)
    for p in range(8):
        x = dot(grad_ref[160 * p : 160 * p + 160, :], weight_ref[...], NT)
        out_ref[p, 0:160, :] = root_code(x * scale[:160, p : p + 1]).astype(BF16)
        out_ref[p, 160:176, :] = sums


def seen_kernel(unit_ref, out_ref):
    row = lax.broadcasted_iota(jnp.int32, (32, 80), 0)
    col = lax.broadcasted_iota(jnp.int32, (32, 80), 1)
    keep = (col // CROPS == row // GLOBAL) & (col % CROPS != row % GLOBAL)
    after = (col // CROPS + 80 // CROPS == row // GLOBAL) & (col % CROPS != row % GLOBAL)
    keep = jnp.where(keep, 1.0, 0.0).astype(BF16)
    after = jnp.where(after, 1.0, 0.0).astype(BF16)
    for j in range(4):
        block = [
            dot(keep, unit_ref[p, :, :256], NN) + dot(after, unit_ref[p, :, 256:], NN)
            for p in range(4 * j, 4 * j + 4)
        ]
        out_ref[:, 128 * j : 128 * j + 128] = jnp.concatenate(block, axis=0).T


def term_kernel(core_ref, unit_ref, grad_ref, came_ref, own_ref, other_ref, total_ref):
    step = pl.program_id(0)
    first = core_ref[0] == 0
    exp_sum = sum_decode(came_ref[0, 32:48, :])
    for p in range(1, 8):
        exp_sum = exp_sum + sum_decode(came_ref[p, 32:48, :])
    exp_sum = jnp.where(step == 0, exp_sum[:8], exp_sum[8:]) * 16.0
    row = lax.broadcasted_iota(jnp.int32, (8, 256), 1)
    weight = jnp.where(row % CROPS < GLOBAL, (GLOBAL - 1) / PAIRS, GLOBAL / PAIRS)
    factor = columns(jnp.where(row < 160, weight / exp_sum, 0.0))
    for j in range(2):
        parts = []
        for p in range(4 * j, 4 * j + 4):
            unit = jnp.concatenate([unit_ref[p, :, :256], unit_ref[p, :, 256:]], axis=0).astype(F32)
            parts.append(unit * factor[:160, p : p + 1])
        hi, lo = split(jnp.concatenate(parts, axis=0))
        grad = grad_ref[640 * j : 640 * j + 640, :]
        x = dot(hi, grad, TN) + dot(lo, grad, TN)
        if j == 0:
            total_ref[...] = x + jnp.where(step == 0, 0.0, total_ref[...])
        else:
            total_ref[...] += x

    @pl.when(step == 1)
    def _():
        left = total_ref[:, :512]
        right = total_ref[:, 512:]
        own_ref[...] = jnp.where(first, left, right)
        other_ref[...] = jnp.where(first, right, left)


VMEM = pl.BlockSpec(memory_space=pltpu.VMEM)
SMEM = pl.BlockSpec(memory_space=pltpu.SMEM)


def call(kernel, shapes, flops, moved, *args, specs=None, room=32, **more):
    if specs is None:
        specs = [SMEM if x.ndim == 1 and x.dtype == jnp.int32 else VMEM for x in args]
    return pl.pallas_call(
        kernel,
        out_shape=shapes,
        in_specs=specs,
        cost_estimate=pl.CostEstimate(flops=flops, bytes_accessed=moved, transcendentals=0),
        compiler_params=pltpu.CompilerParams(vmem_limit_bytes=room * 1024 * 1024),
        **more,
    )(*args)


def shape(dims, dtype=F32):
    return pltpu.HBM(dims, dtype)


def hbm(x):
    return pltpu.with_memory_space_constraint(x, pltpu.HBM)


def shards(student_feat, prototypes, teacher_logits):
    core = lax.axis_index("core")
    core_arg = core.reshape(1)
    chip = lax.axis_index(PLANE)
    block = core * 16 + chip
    place = jnp.stack([chip, lax.axis_index("proto")])

    send = call(
        pack_kernel,
        shape((16, 160, 512), BF16),
        10**7,
        5 * 10**6,
        core_arg,
        teacher_logits,
        prototypes,
        student_feat,
        specs=[
            SMEM,
            pl.BlockSpec((32, 4096), lambda i: (0, i)),
            pl.BlockSpec((8, 4096), lambda i: (0, i)),
            pl.BlockSpec((160, 256), lambda i: (0, 0)),
        ],
        out_specs=pl.BlockSpec((4, 160, 512), lambda i: (i, 0, 0)),
        scratch_shapes=[pltpu.VMEM((80, 512), BF16)],
        grid=(4,),
        room=56,
    )
    got = lax.all_to_all(send, PLANE, 0, 0, tiled=True)
    mate = lax.ppermute(got[:, 32:80], "core", SWAP)
    half = pl.BlockSpec((16, 32, 512), lambda i: (0, 0, 0))

    mass, pack = call(
        first_kernel,
        (shape((512, 1024)), shape((32, 8, 128))),
        10**7,
        3 * 10**6,
        core_arg,
        got,
        mate,
        specs=[SMEM, half, half],
        out_specs=(VMEM, VMEM),
        grid=(1,),
    )
    came = lax.all_to_all(pack, BATCH, 0, 0, tiled=True)
    row_sum = jnp.sum(came, axis=0)
    got, mate, _ = lax.optimization_barrier((got, mate, pack))
    whole = lambda *dims: pl.BlockSpec(dims, lambda i: (0,) * len(dims))
    grad_prob, exp_part, weights, my_weights, my_scale, my_inv, unit_hi, unit_lo = call(
        exp_kernel,
        (
            shape((2560, 1024), BF16),
            shape((16, 256)),
            shape((256, 1024), BF16),
            shape((256, 512), BF16),
            shape((1, 512)),
            shape((1, 512)),
            shape((256, 512), BF16),
            shape((256, 512), BF16),
        ),
        2 * 10**9,
        9 * 10**6,
        core_arg,
        got,
        mate,
        got,
        specs=[
            SMEM,
            pl.BlockSpec((16, 16, 512), lambda i: (0, 4, 0)),
            pl.BlockSpec((16, 16, 512), lambda i: (0, 2, 0)),
            pl.BlockSpec((4, 80, 512), lambda i: (i, 1, 0)),
        ],
        out_specs=(
            pl.BlockSpec((640, 1024), lambda i: (i, 0)),
            whole(16, 256),
            whole(256, 1024),
            whole(256, 512),
            whole(1, 512),
            whole(1, 512),
            whole(256, 512),
            whole(256, 512),
        ),
        scratch_shapes=[pltpu.VMEM((1, 1024), F32)],
        grid=(4,),
    )
    unit_spec = pl.BlockSpec((8, 80, 512), lambda i: (i, 1, 0))

    grad_prob, row_sum = lax.optimization_barrier((grad_prob, row_sum))
    came_one = lax.all_to_all(jnp.broadcast_to(row_sum[None], (8, 8, 128)), "proto", 0, 0, tiled=True)
    student_pack = call(
        student_kernel,
        shape((16, 192, 256), BF16),
        2 * 10**9,
        7 * 10**6,
        hbm(grad_prob),
        weights,
        exp_part,
        exp_part,
        specs=[
            pl.BlockSpec((1280, 1024), lambda i: (i, 0)),
            VMEM,
            pl.BlockSpec((8, 256), lambda i: (i, 0)),
            VMEM,
        ],
        out_specs=pl.BlockSpec((8, 192, 256), lambda i: (i, 0, 0)),
        grid=(2,),
    )
    came_one, student_pack = lax.optimization_barrier((came_one, student_pack))

    part = call(
        second_kernel,
        shape((8, 128)),
        10**7,
        2 * 10**6,
        came_one,
        hbm(mass),
        specs=[VMEM, pl.BlockSpec(memory_space=pltpu.HBM)],
        out_specs=VMEM,
        scratch_shapes=[pltpu.VMEM((512, 1024), F32), pltpu.SemaphoreType.DMA((4,))],
    )
    part_mate = lax.ppermute(part, "core", SWAP)
    pack = call(
        insert_kernel,
        shape((16, 192, 256), BF16),
        10**4,
        10**5,
        part,
        part_mate,
        hbm(student_pack),
        specs=[VMEM, VMEM, pl.BlockSpec(memory_space=pltpu.HBM)],
        out_specs=pl.BlockSpec((16, 16, 256), lambda i: (0, 11, 0)),
        grid=(1,),
        input_output_aliases={2: 0},
    )
    came = lax.all_to_all(pack, PLANE, 0, 0, tiled=True)

    got, _ = lax.optimization_barrier((got, pack))
    seen = call(
        seen_kernel,
        shape((256, 512)),
        10**8,
        2 * 10**6,
        got,
        specs=[pl.BlockSpec((16, 80, 512), lambda i: (0, 1, 0))],
        out_specs=VMEM,
        grid=(1,),
    )
    seen_mate = lax.ppermute(seen, "core", SWAP)

    pack = call(
        home_kernel,
        shape((8, 48, 256), BF16),
        10**7,
        2 * 10**6,
        place,
        hbm(came),
        specs=[SMEM, pl.BlockSpec((4, 192, 256), lambda i: (i, 0, 0))],
        out_specs=pl.BlockSpec((8, 48, 256), lambda i: (0, 0, 0)),
        scratch_shapes=[
            pltpu.VMEM((160, 256), F32),
            pltpu.VMEM((16, 256), F32),
            pltpu.VMEM((8, 256), F32),
            pltpu.VMEM((256, 128), F32),
        ],
        grid=(4,),
    )
    came_two = lax.all_to_all(pack, "proto", 0, 0, tiled=True)

    keep, pack = call(
        third_kernel,
        (shape((512, 1024), BF16), shape((32, 48, 256), BF16)),
        10**9,
        4 * 10**6,
        came_two,
        mass,
        unit_hi,
        unit_lo,
        out_specs=(VMEM, VMEM),
    )
    came = lax.all_to_all(pack, BATCH, 0, 0, tiled=True)

    came_two, _ = lax.optimization_barrier((came_two, pack))
    term, other = call(
        term_kernel,
        (shape((256, 512)), shape((256, 512))),
        3 * 10**9,
        7 * 10**6,
        core_arg,
        got,
        hbm(grad_prob),
        came_two,
        specs=[SMEM, unit_spec, pl.BlockSpec((1280, 1024), lambda i: (i, 0)), VMEM],
        out_specs=(VMEM, VMEM),
        scratch_shapes=[pltpu.VMEM((256, 1024), F32)],
        grid=(2,),
    )
    term_mate = lax.ppermute(other, "core", SWAP)
    home_slice = call(slice_kernel, shape((24, 256)), 10**6, 10**5, place, came_two, out_specs=VMEM)

    pack = call(
        target_kernel,
        shape((8, 64, 256), BF16),
        10**7,
        10**6,
        block.reshape(1),
        came,
        home_slice,
        out_specs=VMEM,
        scratch_shapes=[pltpu.VMEM((128, 128), F32)],
    )
    came = lax.all_to_all(pack, "proto", 0, 0, tiled=True)

    column = pl.BlockSpec((256, 128), lambda i: (0, i))
    line = pl.BlockSpec((1, 128), lambda i: (0, i))
    grad = call(
        final_kernel,
        shape((256, 512)),
        10**9,
        4 * 10**6,
        core_arg,
        came,
        hbm(keep),
        hbm(seen),
        hbm(seen_mate),
        hbm(term),
        hbm(term_mate),
        hbm(my_weights),
        my_scale,
        my_inv,
        specs=[SMEM, VMEM, pl.BlockSpec((128, 1024), lambda i: (i, 0)), VMEM, VMEM, column, column, column, line, line],
        out_specs=column,
        scratch_shapes=[pltpu.VMEM((256, 1024), BF16), pltpu.VMEM((256, 1024), BF16)],
        grid=(4,),
    )
    came, student_feat, _ = lax.optimization_barrier((came, student_feat, grad))
    grad = lax.all_to_all(grad.reshape(32, 8, 512), BATCH, 0, 0, tiled=True)
    grad_weight = grad.transpose(1, 0, 2).reshape(8, 16384)
    grad_feat = call(
        feat_kernel,
        shape((160, 256)),
        10**7,
        10**6,
        block.reshape(1),
        came,
        student_feat,
        out_specs=VMEM,
        scratch_shapes=[pltpu.VMEM((128, 128), F32)],
    )
    return (grad_feat, grad_weight)


def solution(mesh):
    split_mesh = Mesh(mesh.devices.reshape(4, 4, 2, 8), ("y", "x", "core", "proto"))
    return jax.shard_map(
        shards,
        mesh=split_mesh,
        in_specs=(P(BATCH, None), P(BATCH, "proto"), P(BATCH, "proto")),
        out_specs=(P(BATCH, None), P(BATCH, "proto")),
        check_vma=False,
    )
```

```python
import jax
import jax.numpy as jnp
from jax import lax
from jax.experimental import pallas as pl
from jax.experimental.pallas import tpu as pltpu
from jax.sharding import Mesh, PartitionSpec as P

CROPS = 10
GLOBAL = 2
STUDENT_TEMP = 0.1
TEACHER_TEMP = 0.04
PAIRS = float(GLOBAL * CROPS - GLOBAL)
F32 = jnp.float32
BF16 = jnp.bfloat16
PLANE = ("y", "x")
BATCH = ("y", "x", "core")
SWAP = ((0, 1), (1, 0))
SPAN = 250.0
LOW = 125.0
LOG2E = 1.4426950408889634
ROOT = 3276.8
WIDE = 16384.0
TINY = 1e-38


def encode_logits(x):
    mag = jnp.exp2(jnp.abs(x) * SPAN - LOW)
    return jnp.where(x < 0, -mag, mag).astype(BF16)


def decode_exp(code):
    v = code.astype(F32)
    mag = (jnp.log2(jnp.abs(v)) + LOW) * (LOG2E / (TEACHER_TEMP * SPAN))
    return jnp.exp2(jnp.where(v < 0, -mag, mag))


def root_code(x):
    y = x * x
    y = y * y
    return jnp.where(x < 0, -y, y)


def root_decode(code):
    v = code.astype(F32)
    y = lax.rsqrt(lax.rsqrt(jnp.abs(v) + TINY))
    return jnp.where(v < 0, -y, y)


def fine_code(x):
    y = x * x
    y = y * y
    y = y * y
    return jnp.where(x < 0, -y, y)


def fine_decode(code):
    v = code.astype(F32)
    y = jnp.sqrt(lax.rsqrt(lax.rsqrt(jnp.abs(v) + TINY)))
    return jnp.where(v < 0, -y, y)


def sum_code(x):
    y = x * (1.0 / 1024.0)
    y = y * y
    y = y * y
    return y * y


def sum_decode(code):
    return jnp.sqrt(lax.rsqrt(lax.rsqrt(code.astype(F32)))) * 1024.0


def split(x):
    hi = x.astype(BF16)
    return hi, (x - hi.astype(F32)).astype(BF16)


def dot(a, b, dims):
    return lax.dot_general(a, b, (dims, ((), ())), preferred_element_type=F32)


NN = ((1,), (0,))
NT = ((1,), (1,))
TN = ((0,), (0,))


def lanes(x8):
    return jnp.concatenate([x8[i : i + 1] for i in range(8)], axis=1)


def rows8(x):
    return jnp.concatenate([x[:, 128 * i : 128 * (i + 1)] for i in range(8)], axis=0)


def split_row(x8):
    hi = x8.astype(BF16).astype(F32)
    return jnp.concatenate([hi, x8 - hi], axis=1)


def join_row(x):
    return x[:, :128] + x[:, 128:]


def padded(x8):
    return jnp.concatenate([x8, jnp.zeros_like(x8)], axis=0).astype(BF16)


def sweep(mass_ref, row_inv, keep_ref=None, copies=None):
    total = jnp.zeros((8, 1024), F32)
    for low in range(0, 512, 32):
        if copies is not None and low % 64 == 0:
            copies[low // 64].wait()
        x = mass_ref[low : low + 32, :]
        y = x if row_inv is None else x * row_inv
        x = x * (1.0 / jnp.sum(y, axis=1, keepdims=True))
        if keep_ref is not None:
            keep_ref[low : low + 32, :] = x.astype(BF16)
        total = total + ((x[:8] + x[8:16]) + (x[16:24] + x[24:]))
    return jnp.sum(total, axis=0, keepdims=True)


def pack_kernel(core_ref, teacher_ref, proto_ref, feat_ref, out_ref, unit_ref):
    first = core_ref[0] == 0

    @pl.when(pl.program_id(0) == 0)
    def _():
        x = feat_ref[...].astype(F32)
        unit = x / jnp.sqrt(jnp.sum(x * x, axis=1, keepdims=True) + 1e-06)
        unit = unit.astype(BF16)
        unit_ref[:, :256] = unit[:80]
        unit_ref[:, 256:] = unit[80:]

    for p in range(8):
        left = encode_logits(teacher_ref[:, 1024 * p : 1024 * p + 512])
        right = encode_logits(teacher_ref[:, 1024 * p + 512 : 1024 * p + 1024])
        out_ref[p, 0:32, :] = jnp.where(first, left, right)
        out_ref[p, 32:64, :] = jnp.where(first, right, left)
        w = proto_ref[:, 1024 * p : 1024 * p + 1024].astype(F32)
        out_ref[p, 64:80, :] = jnp.concatenate([w[:, :512], w[:, 512:]], axis=0).astype(BF16)
        out_ref[p, 80:160, :] = unit_ref[...]


def first_kernel(core_ref, own_ref, mate_ref, mass_ref, out_ref):
    first = core_ref[0] == 0
    for j in range(4):
        own = decode_exp(own_ref[4 * j : 4 * j + 4].reshape(128, 512)).T
        mate = decode_exp(mate_ref[4 * j : 4 * j + 4].reshape(128, 512)).T
        mass_ref[:, 128 * j : 128 * j + 128] = jnp.where(first, own, mate)
        mass_ref[:, 512 + 128 * j : 640 + 128 * j] = jnp.where(first, mate, own)
    part = rows8(sweep(mass_ref, None))
    out_ref[...] = jnp.broadcast_to(part[None], (32, 8, 128))


def second_kernel(came_ref, mass_hbm, pack_ref, out_ref, mass_ref, sems):
    copies = [
        pltpu.make_async_copy(mass_hbm.at[pl.ds(64 * i, 64), :], mass_ref.at[pl.ds(64 * i, 64), :], sems.at[i])
        for i in range(8)
    ]
    for copy in copies:
        copy.start()
    row_inv = lanes(1.0 / jnp.sum(came_ref[...], axis=0))
    row = padded(split_row(rows8(sweep(mass_ref, row_inv, copies=copies))))
    out_ref[...] = jnp.broadcast_to(row[None], (16, 16, 256))


def home_kernel(place_ref, came_ref, out_ref):
    pick = lax.broadcasted_iota(jnp.int32, (16, 256), 0) == place_ref[0]
    exp_sum = jnp.zeros((16, 256), F32)
    row_sum = jnp.zeros((8, 256), F32)
    parts = []
    for p in range(16):
        exp_part = sum_decode(came_ref[p, 160:176, :])
        exp_sum = exp_sum + exp_part
        row_sum = row_sum + came_ref[p, 176:192, :].astype(F32)[:8]
        parts.append(jnp.sum(jnp.where(pick, exp_part, 0.0), axis=0, keepdims=True))
    parts = columns(jnp.concatenate(parts, axis=0) * (1.0 / ROOT))
    scale = 1.0 / jnp.sum(parts, axis=1, keepdims=True)
    code = []
    for low in range(0, 160, 32):
        home = jnp.zeros((32, 256), F32)
        for p in range(16):
            home = home + root_decode(came_ref[p, low : low + 32, :]) * parts[low : low + 32, p : p + 1]
        code.append(fine_code(home * scale[low : low + 32]))
    code = jnp.concatenate(code, axis=0)
    tail = [jnp.zeros((4, 256), F32), split_row(join_row(row_sum)), sum_code(exp_sum * (1.0 / 16.0))]
    for z in range(8):
        out_ref[z] = jnp.concatenate([code[20 * z : 20 * z + 20]] + tail, axis=0).astype(BF16)


def slice_kernel(place_ref, came_ref, out_ref):
    pick = lax.broadcasted_iota(jnp.int32, (16, 256), 0) == place_ref[0]
    parts = []
    for p in range(8):
        exp_part = sum_decode(came_ref[p, 32:48, :]) * 16.0
        parts.append(jnp.sum(jnp.where(pick, exp_part, 0.0), axis=0, keepdims=True))
    parts = pltpu.roll(jnp.concatenate(parts, axis=0), (256 - 20 * place_ref[1]) % 256, 1)
    parts = columns(parts)[:32]
    home = jnp.zeros((32, 256), F32)
    for p in range(8):
        home = home + fine_decode(came_ref[p, 0:32, :]) * parts[:, p : p + 1]
    row = lax.broadcasted_iota(jnp.int32, (32, 1), 0)
    weight = jnp.where(row % CROPS < GLOBAL, (GLOBAL - 1) / PAIRS, GLOBAL / PAIRS) * (WIDE / ROOT)
    out_ref[...] = fine_code(home * (weight / jnp.sum(parts, axis=1, keepdims=True)))[:24]


def third_kernel(came_ref, came_mate_ref, mass_ref, hi_ref, lo_ref, keep_ref, out_ref):
    rows = jnp.zeros((16, 256), F32)
    for p in range(8):
        rows = rows + (came_ref[p, 16:32, :].astype(F32) + came_mate_ref[p, 16:32, :].astype(F32))
    row_inv = lanes(1.0 / join_row(rows[8:]))
    part = sweep(mass_ref, row_inv, keep_ref)
    scale = ROOT / part
    tail = split_row(rows8(part))
    for j in range(8):
        keep = keep_ref[:, 128 * j : 128 * j + 128]
        x = jnp.dot(hi_ref[...], keep, preferred_element_type=F32)
        x = x + jnp.dot(lo_ref[...], keep, preferred_element_type=F32)
        x = (x * scale[:, 128 * j : 128 * j + 128]).T
        x = root_code(x)
        for i in range(4):
            block = 4 * j + i
            out_ref[block % 16 * 2 + block // 16] = jnp.concatenate([x[32 * i : 32 * i + 32], tail], axis=0).astype(BF16)


def target_kernel(index_ref, came_ref, slice_ref, out_ref, turn_ref):
    index = index_ref[0]
    pick = lax.broadcasted_iota(jnp.int32, (8, 128), 0) == index // 4
    row_sum = jnp.zeros((8, 128), F32)
    parts = []
    for p in range(32):
        row = join_row(came_ref[p].astype(F32)[32:])
        row_sum = row_sum + row
        parts.append(jnp.sum(jnp.where(pick, row, 0.0), axis=0, keepdims=True))
    parts = jnp.concatenate(parts, axis=0) * (1.0 / ROOT)
    turn_ref[...] = jnp.concatenate([parts, jnp.zeros((96, 128), F32)], axis=0).T
    parts = turn_ref[pl.ds(pl.multiple_of(index % 4 * 32, 32), 32), :]
    total = jnp.zeros((32, 256), F32)
    for p in range(32):
        total = total + root_decode(came_ref[p])[:32] * parts[:, p : p + 1]
    code = fine_code(total / jnp.sum(parts, axis=1, keepdims=True))
    code = jnp.concatenate([code, slice_ref[...], split_row(row_sum)], axis=0).astype(BF16)
    out_ref[...] = jnp.broadcast_to(code[None], (8, 64, 256))


def feat_kernel(index_ref, came_ref, feat_ref, out_ref, turn_ref):
    index = index_ref[0]
    pick = lax.broadcasted_iota(jnp.int32, (8, 128), 0) == index // 4
    parts = []
    for p in range(8):
        row = join_row(came_ref[p, 48:64, :].astype(F32)[8:])
        parts.append(jnp.sum(jnp.where(pick, row, 0.0), axis=0, keepdims=True))
    parts = jnp.concatenate(parts + [jnp.zeros((120, 128), F32)], axis=0)
    turn_ref[...] = parts.T
    parts = turn_ref[pl.ds(pl.multiple_of(index % 4 * 32, 32), 32), :]
    target = jnp.zeros((32, 256), F32)
    for p in range(8):
        target = target + fine_decode(came_ref[p, 0:32, :]) * parts[:, p : p + 1]
    target = target / jnp.sum(parts, axis=1, keepdims=True) * (1.0 / (ROOT * PAIRS))
    hi, lo = split(target)
    row = lax.broadcasted_iota(jnp.int32, (160, 32), 0)
    col = lax.broadcasted_iota(jnp.int32, (160, 32), 1)
    keep = jnp.where((row // CROPS == col // GLOBAL) & (row % CROPS != col % GLOBAL), 1.0, 0.0).astype(BF16)
    student = [fine_decode(came_ref[p, 32:64, :])[:20] for p in range(8)]
    total = jnp.concatenate(student, axis=0) * (1.0 / WIDE) - (dot(keep, hi, NN) + dot(keep, lo, NN))
    x = feat_ref[...].astype(F32)
    norm = jnp.sqrt(jnp.sum(x * x, axis=1, keepdims=True) + 1e-06)
    unit = x / norm
    out_ref[...] = (total - unit * jnp.sum(unit * total, axis=1, keepdims=True)) / norm


def final_kernel(
    core_ref, came_ref, keep_ref, seen_ref, mate_ref, term_ref, term_mate_ref, weight_ref, scale_ref, inv_ref, out_ref
):
    first = core_ref[0] == 0
    rows = came_ref[0, 48:64, :].astype(F32)
    for p in range(1, 8):
        rows = rows + came_ref[p, 48:64, :].astype(F32)
    row_inv = lanes(1.0 / join_row(rows[8:])) * (1.0 / PAIRS)
    seen = seen_ref[...]
    mate = mate_ref[...]
    low_hi, low_lo = split(jnp.where(first, seen, mate) * row_inv[:, :512])
    high_hi, high_lo = split(jnp.where(first, mate, seen) * row_inv[:, 512:])
    for j in range(4):
        cols = slice(128 * j, 128 * j + 128)
        keep = keep_ref[cols, :]
        x = dot(low_hi, keep[:, :512], NT) + dot(low_lo, keep[:, :512], NT)
        x = x + (dot(high_hi, keep[:, 512:], NT) + dot(high_lo, keep[:, 512:], NT))
        x = term_ref[:, cols] + term_mate_ref[:, cols] - x * scale_ref[:, cols]
        w = weight_ref[:, cols].astype(F32)
        dots = jnp.sum(w * x, axis=0, keepdims=True) * inv_ref[:, cols]
        out_ref[:, cols] = x - w * dots


def columns(x):
    return jnp.concatenate([x, jnp.zeros((128 - x.shape[0], 256), F32)], axis=0).T


def exp_kernel(
    core_ref, own_ref, mate_ref, unit_ref, out_ref, sum_ref, all_ref, my_ref, my_scale_ref, my_inv_ref, hi_ref, lo_ref,
    scale_ref,
):
    step = pl.program_id(0)

    @pl.when(step == 0)
    def _():
        first = core_ref[0] == 0
        squares = jnp.zeros((8, 1024), F32)
        for p in range(16):
            own = own_ref[p].astype(F32)
            mate = mate_ref[p].astype(F32)
            low = jnp.where(first, own, mate)
            high = jnp.where(first, mate, own)
            left = jnp.concatenate([low[:8], high[:8]], axis=0)
            right = jnp.concatenate([low[8:], high[8:]], axis=0)
            rows = slice(16 * p, 16 * p + 16)
            all_ref[rows, :512] = left.astype(BF16)
            all_ref[rows, 512:] = right.astype(BF16)
            my_ref[rows, :] = jnp.where(first, left, right).astype(BF16)
            both = jnp.concatenate([left, right], axis=1)
            both = both * both
            squares = squares + (both[:8] + both[8:])
        norm_sq = jnp.sum(squares, axis=0, keepdims=True) + 1e-06
        scale = 1.0 / (jnp.sqrt(norm_sq) * STUDENT_TEMP)
        scale_ref[...] = scale
        my_inv_ref[...] = 1.0 / jnp.where(first, norm_sq[:, :512], norm_sq[:, 512:])
        my_scale = jnp.where(first, scale[:, :512], scale[:, 512:])
        my_scale_ref[...] = my_scale
        for p in range(8):
            rows = slice(32 * p, 32 * p + 32)
            hi, lo = split(my_ref[rows, :].astype(F32) * my_scale)
            hi_ref[rows, :] = hi
            lo_ref[rows, :] = lo

    scale = scale_ref[...]
    power = scale * LOG2E
    sums = []
    for p in range(4):
        for half in range(2):
            raw = dot(unit_ref[p, :, 256 * half : 256 * half + 256], all_ref[...], NN)
            prob = jnp.exp2(raw * power)
            sums.append(jnp.sum(prob, axis=1, keepdims=True))
            out_ref[160 * p + 80 * half : 160 * p + 80 * half + 80, :] = (prob * scale).astype(BF16)
    sums = [jnp.concatenate(sums[2 * p : 2 * p + 2], axis=0) for p in range(4)]
    sums = jnp.concatenate(sums + [jnp.ones((160, 124), F32)], axis=1)
    sums = jnp.concatenate([sums, jnp.ones((96, 128), F32)], axis=0).T[:4]
    row = lax.broadcasted_iota(jnp.int32, (16, 256), 0)
    sum_ref[...] = jnp.where(row // 4 == step, jnp.concatenate([sums] * 4, axis=0), sum_ref[...])


def student_kernel(grad_ref, weight_ref, part_ref, sum_ref, out_ref):
    scale = columns(ROOT / part_ref[...])
    sums = sum_code(sum_ref[...]).astype(BF16)
    for p in range(8):
        x = dot(grad_ref[160 * p : 160 * p + 160, :], weight_ref[...], NT)
        out_ref[p, 0:160, :] = root_code(x * scale[:160, p : p + 1]).astype(BF16)
        out_ref[p, 160:176, :] = sums


def seen_kernel(unit_ref, out_ref):
    row = lax.broadcasted_iota(jnp.int32, (32, 80), 0)
    col = lax.broadcasted_iota(jnp.int32, (32, 80), 1)
    keep = (col // CROPS == row // GLOBAL) & (col % CROPS != row % GLOBAL)
    after = (col // CROPS + 80 // CROPS == row // GLOBAL) & (col % CROPS != row % GLOBAL)
    keep = jnp.where(keep, 1.0, 0.0).astype(BF16)
    after = jnp.where(after, 1.0, 0.0).astype(BF16)
    for j in range(4):
        block = [
            dot(keep, unit_ref[p, :, :256], NN) + dot(after, unit_ref[p, :, 256:], NN)
            for p in range(4 * j, 4 * j + 4)
        ]
        out_ref[:, 128 * j : 128 * j + 128] = jnp.concatenate(block, axis=0).T


def term_kernel(core_ref, unit_ref, grad_ref, came_ref, own_ref, other_ref, total_ref):
    step = pl.program_id(0)
    first = core_ref[0] == 0
    exp_sum = sum_decode(came_ref[0, 32:48, :])
    for p in range(1, 8):
        exp_sum = exp_sum + sum_decode(came_ref[p, 32:48, :])
    exp_sum = jnp.where(step == 0, exp_sum[:8], exp_sum[8:]) * 16.0
    row = lax.broadcasted_iota(jnp.int32, (8, 256), 1)
    weight = jnp.where(row % CROPS < GLOBAL, (GLOBAL - 1) / PAIRS, GLOBAL / PAIRS)
    factor = columns(jnp.where(row < 160, weight / exp_sum, 0.0))
    for j in range(2):
        parts = []
        for p in range(4 * j, 4 * j + 4):
            unit = jnp.concatenate([unit_ref[p, :, :256], unit_ref[p, :, 256:]], axis=0).astype(F32)
            parts.append(unit * factor[:160, p : p + 1])
        hi, lo = split(jnp.concatenate(parts, axis=0))
        grad = grad_ref[640 * j : 640 * j + 640, :]
        x = dot(hi, grad, TN) + dot(lo, grad, TN)
        if j == 0:
            total_ref[...] = x + jnp.where(step == 0, 0.0, total_ref[...])
        else:
            total_ref[...] += x

    @pl.when(step == 1)
    def _():
        left = total_ref[:, :512]
        right = total_ref[:, 512:]
        own_ref[...] = jnp.where(first, left, right)
        other_ref[...] = jnp.where(first, right, left)


VMEM = pl.BlockSpec(memory_space=pltpu.VMEM)
SMEM = pl.BlockSpec(memory_space=pltpu.SMEM)


def call(kernel, shapes, flops, moved, *args, specs=None, room=32, **more):
    if specs is None:
        specs = [SMEM if x.ndim == 1 and x.dtype == jnp.int32 else VMEM for x in args]
    return pl.pallas_call(
        kernel,
        out_shape=shapes,
        in_specs=specs,
        cost_estimate=pl.CostEstimate(flops=flops, bytes_accessed=moved, transcendentals=0),
        compiler_params=pltpu.CompilerParams(vmem_limit_bytes=room * 1024 * 1024),
        **more,
    )(*args)


def shape(dims, dtype=F32):
    return pltpu.HBM(dims, dtype)


def hbm(x):
    return pltpu.with_memory_space_constraint(x, pltpu.HBM)


def shards(student_feat, prototypes, teacher_logits):
    core = lax.axis_index("core")
    core_arg = core.reshape(1)
    chip = lax.axis_index(PLANE)
    block = core * 16 + chip
    place = jnp.stack([chip, lax.axis_index("proto")])

    send = call(
        pack_kernel,
        shape((16, 160, 512), BF16),
        10**7,
        5 * 10**6,
        core_arg,
        teacher_logits,
        prototypes,
        student_feat,
        specs=[
            SMEM,
            pl.BlockSpec((32, 8192), lambda i: (0, i)),
            pl.BlockSpec((8, 8192), lambda i: (0, i)),
            pl.BlockSpec((160, 256), lambda i: (0, 0)),
        ],
        out_specs=pl.BlockSpec((8, 160, 512), lambda i: (i, 0, 0)),
        scratch_shapes=[pltpu.VMEM((80, 512), BF16)],
        grid=(2,),
        room=56,
    )
    got = lax.all_to_all(send, PLANE, 0, 0, tiled=True)
    mate = lax.ppermute(got[:, 32:80], "core", SWAP)
    half = pl.BlockSpec((16, 32, 512), lambda i: (0, 0, 0))

    mass, pack = call(
        first_kernel,
        (shape((512, 1024)), shape((32, 8, 128))),
        10**7,
        3 * 10**6,
        core_arg,
        got,
        mate,
        specs=[SMEM, half, half],
        out_specs=(VMEM, VMEM),
        grid=(1,),
    )
    came = lax.all_to_all(pack, BATCH, 0, 0, tiled=True)
    row_sum = jnp.sum(came, axis=0)
    got, mate, _ = lax.optimization_barrier((got, mate, pack))
    whole = lambda *dims: pl.BlockSpec(dims, lambda i: (0,) * len(dims))
    grad_prob, exp_part, weights, my_weights, my_scale, my_inv, unit_hi, unit_lo = call(
        exp_kernel,
        (
            shape((2560, 1024), BF16),
            shape((16, 256)),
            shape((256, 1024), BF16),
            shape((256, 512), BF16),
            shape((1, 512)),
            shape((1, 512)),
            shape((256, 512), BF16),
            shape((256, 512), BF16),
        ),
        2 * 10**9,
        9 * 10**6,
        core_arg,
        got,
        mate,
        got,
        specs=[
            SMEM,
            pl.BlockSpec((16, 16, 512), lambda i: (0, 4, 0)),
            pl.BlockSpec((16, 16, 512), lambda i: (0, 2, 0)),
            pl.BlockSpec((4, 80, 512), lambda i: (i, 1, 0)),
        ],
        out_specs=(
            pl.BlockSpec((640, 1024), lambda i: (i, 0)),
            whole(16, 256),
            whole(256, 1024),
            whole(256, 512),
            whole(1, 512),
            whole(1, 512),
            whole(256, 512),
            whole(256, 512),
        ),
        scratch_shapes=[pltpu.VMEM((1, 1024), F32)],
        grid=(4,),
    )
    unit_spec = pl.BlockSpec((8, 80, 512), lambda i: (i, 1, 0))

    grad_prob, row_sum = lax.optimization_barrier((grad_prob, row_sum))
    came_one = lax.all_to_all(jnp.broadcast_to(row_sum[None], (8, 8, 128)), "proto", 0, 0, tiled=True)
    student_pack = call(
        student_kernel,
        shape((16, 192, 256), BF16),
        2 * 10**9,
        7 * 10**6,
        hbm(grad_prob),
        hbm(weights),
        exp_part,
        exp_part,
        specs=[
            pl.BlockSpec((1280, 1024), lambda i: (i, 0)),
            whole(256, 1024),
            pl.BlockSpec((8, 256), lambda i: (i, 0)),
            VMEM,
        ],
        out_specs=pl.BlockSpec((8, 192, 256), lambda i: (i, 0, 0)),
        grid=(2,),
    )
    came_one, student_pack = lax.optimization_barrier((came_one, student_pack))

    pack = call(
        second_kernel,
        shape((16, 192, 256), BF16),
        10**7,
        2 * 10**6,
        came_one,
        hbm(mass),
        hbm(student_pack),
        specs=[VMEM, pl.BlockSpec(memory_space=pltpu.HBM), pl.BlockSpec(memory_space=pltpu.HBM)],
        out_specs=pl.BlockSpec((16, 16, 256), lambda i: (0, 11, 0)),
        scratch_shapes=[pltpu.VMEM((512, 1024), F32), pltpu.SemaphoreType.DMA((8,))],
        grid=(1,),
        input_output_aliases={2: 0},
    )
    came = lax.all_to_all(pack, PLANE, 0, 0, tiled=True)

    got, _ = lax.optimization_barrier((got, pack))
    seen = call(
        seen_kernel,
        shape((256, 512)),
        10**8,
        2 * 10**6,
        got,
        specs=[pl.BlockSpec((16, 80, 512), lambda i: (0, 1, 0))],
        out_specs=VMEM,
        grid=(1,),
    )
    seen_mate = lax.ppermute(seen, "core", SWAP)

    pack = call(
        home_kernel,
        shape((8, 48, 256), BF16),
        10**7,
        2 * 10**6,
        place,
        hbm(came),
        specs=[SMEM, whole(16, 192, 256)],
        out_specs=whole(8, 48, 256),
        grid=(1,),
    )
    came_two = lax.all_to_all(pack, "proto", 0, 0, tiled=True)

    keep, pack = call(
        third_kernel,
        (shape((512, 1024), BF16), shape((32, 40, 256), BF16)),
        10**9,
        4 * 10**6,
        came_two,
        lax.ppermute(came_two, "core", SWAP),
        mass,
        unit_hi,
        unit_lo,
        out_specs=(VMEM, VMEM),
    )
    came = lax.all_to_all(pack, BATCH, 0, 0, tiled=True)

    came_two, _ = lax.optimization_barrier((came_two, pack))
    term, other = call(
        term_kernel,
        (shape((256, 512)), shape((256, 512))),
        3 * 10**9,
        7 * 10**6,
        core_arg,
        got,
        hbm(grad_prob),
        came_two,
        specs=[SMEM, unit_spec, pl.BlockSpec((1280, 1024), lambda i: (i, 0)), VMEM],
        out_specs=(VMEM, VMEM),
        scratch_shapes=[pltpu.VMEM((256, 1024), F32)],
        grid=(2,),
    )
    term_mate = lax.ppermute(other, "core", SWAP)
    home_slice = call(slice_kernel, shape((24, 256)), 10**6, 10**5, place, came_two, out_specs=VMEM)

    pack = call(
        target_kernel,
        shape((8, 64, 256), BF16),
        10**7,
        10**6,
        block.reshape(1),
        came,
        home_slice,
        out_specs=VMEM,
        scratch_shapes=[pltpu.VMEM((128, 128), F32)],
    )
    came = lax.all_to_all(pack, "proto", 0, 0, tiled=True)

    grad = call(
        final_kernel,
        shape((256, 512)),
        10**9,
        4 * 10**6,
        core_arg,
        came,
        hbm(keep),
        hbm(seen),
        hbm(seen_mate),
        hbm(term),
        hbm(term_mate),
        hbm(my_weights),
        my_scale,
        my_inv,
        specs=[SMEM, VMEM, whole(512, 1024)] + [whole(256, 512)] * 5 + [VMEM, VMEM],
        out_specs=whole(256, 512),
        grid=(1,),
    )
    came, student_feat, _ = lax.optimization_barrier((came, student_feat, grad))
    grad = lax.all_to_all(grad.reshape(32, 8, 512), BATCH, 0, 0, tiled=True)
    grad_weight = grad.transpose(1, 0, 2).reshape(8, 16384)
    grad_feat = call(
        feat_kernel,
        shape((160, 256)),
        10**7,
        10**6,
        block.reshape(1),
        came,
        student_feat,
        out_specs=VMEM,
        scratch_shapes=[pltpu.VMEM((128, 128), F32)],
    )
    return (grad_feat, grad_weight)


def solution(mesh):
    split_mesh = Mesh(mesh.devices.reshape(4, 4, 2, 8), ("y", "x", "core", "proto"))
    return jax.shard_map(
        shards,
        mesh=split_mesh,
        in_specs=(P(BATCH, None), P(BATCH, "proto"), P(BATCH, "proto")),
        out_specs=(P(BATCH, None), P(BATCH, "proto")),
        check_vma=False,
    )
```

```python
import jax
import jax.numpy as jnp
from jax import lax
from jax.experimental import pallas as pl
from jax.experimental.pallas import tpu as pltpu
from jax.sharding import Mesh, PartitionSpec as P

CROPS = 10
GLOBAL = 2
STUDENT_TEMP = 0.1
TEACHER_TEMP = 0.04
PAIRS = float(GLOBAL * CROPS - GLOBAL)
F32 = jnp.float32
BF16 = jnp.bfloat16
PLANE = ("y", "x")
BATCH = ("y", "x", "core")
SWAP = ((0, 1), (1, 0))
SPAN = 250.0
LOW = 125.0
LOG2E = 1.4426950408889634
ROOT = 3276.8
WIDE = 16384.0
TINY = 1e-38


def encode_logits(x):
    mag = jnp.exp2(jnp.abs(x) * SPAN - LOW)
    return jnp.where(x < 0, -mag, mag).astype(BF16)


def decode_exp(code):
    v = code.astype(F32)
    mag = (jnp.log2(jnp.abs(v)) + LOW) * (LOG2E / (TEACHER_TEMP * SPAN))
    return jnp.exp2(jnp.where(v < 0, -mag, mag))


def root_code(x):
    y = x * x
    y = y * y
    return jnp.where(x < 0, -y, y)


def root_decode(code):
    v = code.astype(F32)
    y = lax.rsqrt(lax.rsqrt(jnp.abs(v) + TINY))
    return jnp.where(v < 0, -y, y)


def fine_code(x):
    y = x * x
    y = y * y
    y = y * y
    return jnp.where(x < 0, -y, y)


def fine_decode(code):
    v = code.astype(F32)
    y = jnp.sqrt(lax.rsqrt(lax.rsqrt(jnp.abs(v) + TINY)))
    return jnp.where(v < 0, -y, y)


def sum_code(x):
    y = x * (1.0 / 1024.0)
    y = y * y
    y = y * y
    return y * y


def sum_decode(code):
    return jnp.sqrt(lax.rsqrt(lax.rsqrt(code.astype(F32)))) * 1024.0


def split(x):
    hi = x.astype(BF16)
    return hi, (x - hi.astype(F32)).astype(BF16)


def dot(a, b, dims):
    return lax.dot_general(a, b, (dims, ((), ())), preferred_element_type=F32)


NN = ((1,), (0,))
NT = ((1,), (1,))
TN = ((0,), (0,))


def lanes(x8):
    return jnp.concatenate([x8[i : i + 1] for i in range(8)], axis=1)


def rows8(x):
    return jnp.concatenate([x[:, 128 * i : 128 * (i + 1)] for i in range(8)], axis=0)


def split_row(x8):
    hi = x8.astype(BF16).astype(F32)
    return jnp.concatenate([hi, x8 - hi], axis=1)


def join_row(x):
    return x[:, :128] + x[:, 128:]


def padded(x8):
    return jnp.concatenate([x8, jnp.zeros_like(x8)], axis=0).astype(BF16)


def sweep(mass_ref, row_inv, keep_ref=None, copies=None):
    total = jnp.zeros((8, 1024), F32)
    for low in range(0, 512, 32):
        if copies is not None and low % 64 == 0:
            copies[low // 64].wait()
        x = mass_ref[low : low + 32, :]
        y = x if row_inv is None else x * row_inv
        x = x * (1.0 / jnp.sum(y, axis=1, keepdims=True))
        if keep_ref is not None:
            keep_ref[low : low + 32, :] = x.astype(BF16)
        total = total + ((x[:8] + x[8:16]) + (x[16:24] + x[24:]))
    return jnp.sum(total, axis=0, keepdims=True)


def pack_kernel(teacher_ref, proto_ref, feat_ref, out_ref, unit_ref):
    @pl.when(pl.program_id(0) == 0)
    def _():
        x = feat_ref[...].astype(F32)
        unit = x / jnp.sqrt(jnp.sum(x * x, axis=1, keepdims=True) + 1e-06)
        unit_ref[...] = unit.astype(BF16)

    for p in range(16):
        cols = 512 * p
        out_ref[p, 0:32, :] = encode_logits(teacher_ref[:, cols : cols + 256]).astype(BF16)
        out_ref[p, 32:64, :] = encode_logits(teacher_ref[:, cols + 256 : cols + 512]).astype(BF16)
        w = proto_ref[:, cols : cols + 512].astype(F32)
        out_ref[p, 64:80, :] = jnp.concatenate([w[:, :256], w[:, 256:]], axis=0).astype(BF16)
        out_ref[p, 80:160, :] = unit_ref[80 * (p % 2) : 80 * (p % 2) + 80, :]


def first_kernel(own_ref, mass_ref, out_ref):
    for h in range(2):
        for j in range(4):
            cols = slice(512 * h + 128 * j, 512 * h + 128 * j + 128)
            for side in range(2):
                low = 32 * side + 16 * h
                block = own_ref[8 * j : 8 * j + 8, low : low + 16, :].reshape(128, 256)
                mass_ref[256 * side : 256 * side + 256, cols] = decode_exp(block).T
    part = rows8(sweep(mass_ref, None))
    out_ref[...] = jnp.broadcast_to(part[None], (32, 8, 128))


def second_kernel(came_ref, sum_ref, mass_hbm, pack_ref, out_ref, mass_ref, sems):
    copies = [
        pltpu.make_async_copy(mass_hbm.at[pl.ds(64 * i, 64), :], mass_ref.at[pl.ds(64 * i, 64), :], sems.at[i])
        for i in range(8)
    ]
    for copy in copies:
        copy.start()
    row_inv = lanes(1.0 / jnp.sum(came_ref[...], axis=0))
    part = rows8(sweep(mass_ref, row_inv, copies=copies) * row_inv)
    part = root_code(part * WIDE)
    part = jnp.concatenate([part[:, :64], part[:, 64:]], axis=0)
    row = jnp.concatenate([sum_code(sum_ref[...])[:, :192], part], axis=1).astype(BF16)
    out_ref[...] = jnp.broadcast_to(row[None], (32, 16, 256))


def home_kernel(place_ref, came_ref, out_ref):
    core = place_ref[2]
    pick = lax.broadcasted_iota(jnp.int32, (16, 256), 0) == place_ref[0]
    row_sum = jnp.zeros((16, 256), F32)
    parts = [[], []]
    for p in range(32):
        row_sum = row_sum + root_decode(came_ref[p, 80:96, :])
        exp_part = sum_decode(came_ref[p, 80:96, :])
        parts[p % 2].append(jnp.sum(jnp.where(pick, exp_part, 0.0), axis=0, keepdims=True))
    exp_sum = jnp.zeros((16, 256), F32)
    for p in range(16):
        exp_sum = exp_sum + sum_decode(came_ref[2 * p + core, 80:96, :])
    code = []
    home_sum = []
    for half in range(2):
        x = jnp.concatenate(parts[half], axis=0)
        x = jnp.where(core == 0, x[:, :80], x[:, 80:160])
        home_sum.append(jnp.sum(x, axis=0, keepdims=True))
        x = jnp.concatenate([x, jnp.ones((16, 176), F32)], axis=1)
        x = columns(x * (1.0 / ROOT))[:80]
        scale = 1.0 / jnp.sum(x, axis=1, keepdims=True)
        for low in range(0, 80, 16):
            home = jnp.zeros((16, 256), F32)
            for p in range(16):
                part = root_decode(came_ref[2 * p + half, low : low + 16, :])
                home = home + part * x[low : low + 16, p : p + 1]
            code.append(fine_code(home * scale[low : low + 16]))
    code = jnp.concatenate(code, axis=0)
    home_sum = jnp.concatenate(home_sum + [jnp.ones((1, 96), F32)], axis=1)
    row_sum = jnp.concatenate([row_sum[:8, 192:], row_sum[8:, 192:]], axis=1)
    lane = lax.broadcasted_iota(jnp.int32, (16, 256), 1)
    exp_sum = jnp.where(lane < 160, exp_sum, 1.0)
    tail = [
        sum_code(home_sum * (1.0 / 16.0)),
        jnp.zeros((3, 256), F32),
        split_row(row_sum),
        sum_code(exp_sum * (1.0 / 16.0)),
    ]
    for z in range(8):
        out_ref[z] = jnp.concatenate([code[20 * z : 20 * z + 20]] + tail, axis=0).astype(BF16)


def slice_kernel(place_ref, came_ref, out_ref):
    parts = [sum_decode(came_ref[p, 16:32, :])[4:5] * 16.0 for p in range(8)]
    parts = pltpu.roll(jnp.concatenate(parts, axis=0), (256 - 20 * place_ref[1]) % 256, 1)
    parts = columns(parts)[:32]
    home = jnp.zeros((32, 256), F32)
    for p in range(8):
        home = home + fine_decode(came_ref[p, 0:32, :]) * parts[:, p : p + 1]
    row = lax.broadcasted_iota(jnp.int32, (32, 1), 0)
    weight = jnp.where(row % CROPS < GLOBAL, (GLOBAL - 1) / PAIRS, GLOBAL / PAIRS) * (WIDE / ROOT)
    out_ref[...] = fine_code(home * (weight / jnp.sum(parts, axis=1, keepdims=True)))[:24]


def third_kernel(came_ref, came_one_ref, mass_ref, hi_ref, lo_ref, keep_ref, out_ref):
    rows = jnp.zeros((16, 256), F32)
    for p in range(8):
        rows = rows + came_ref[p, 16:32, :].astype(F32)
    row_inv = lanes(WIDE / (join_row(rows[8:]) * jnp.sum(came_one_ref[...], axis=0)))
    part = sweep(mass_ref, row_inv, keep_ref)
    scale = ROOT / part
    tail = split_row(rows8(part))
    for j in range(4):
        both = []
        for h in range(2):
            cols = slice(512 * h + 128 * j, 512 * h + 128 * j + 128)
            keep = keep_ref[:, cols]
            x = jnp.dot(hi_ref[...], keep, preferred_element_type=F32)
            x = x + jnp.dot(lo_ref[...], keep, preferred_element_type=F32)
            both.append(root_code((x * scale[:, cols]).T))
        for i in range(8):
            rows = slice(16 * i, 16 * i + 16)
            out_ref[8 * j + i] = jnp.concatenate([both[0][rows], both[1][rows], tail], axis=0).astype(BF16)


def home_columns(rows, index, turn_ref):
    pick = lax.broadcasted_iota(jnp.int32, (8, 128), 0) - index // 8
    pad = jnp.zeros((128 - len(rows), 128), F32)
    both = []
    for h in range(2):
        picked = [jnp.sum(jnp.where(pick == 4 * h, row, 0.0), axis=0, keepdims=True) for row in rows]
        turn_ref[...] = jnp.concatenate(picked + [pad], axis=0).T
        both.append(turn_ref[pl.ds(pl.multiple_of(index % 8 * 16, 16), 16), :])
    return jnp.concatenate(both, axis=0)


def target_kernel(index_ref, came_ref, slice_ref, out_ref, turn_ref):
    rows = [join_row(came_ref[p].astype(F32)[32:]) for p in range(32)]
    row_sum = rows[0]
    for p in range(1, 32):
        row_sum = row_sum + rows[p]
    parts = home_columns(rows, index_ref[0], turn_ref) * (1.0 / ROOT)
    total = jnp.zeros((32, 256), F32)
    for p in range(32):
        total = total + root_decode(came_ref[p])[:32] * parts[:, p : p + 1]
    code = fine_code(total / jnp.sum(parts, axis=1, keepdims=True))
    code = jnp.concatenate([code, slice_ref[...], split_row(row_sum)], axis=0).astype(BF16)
    out_ref[...] = jnp.broadcast_to(code[None], (8, 64, 256))


def feat_kernel(index_ref, came_ref, feat_ref, out_ref, turn_ref):
    rows = [join_row(came_ref[p, 48:64, :].astype(F32)[8:]) for p in range(8)]
    parts = home_columns(rows, index_ref[0], turn_ref)
    target = jnp.zeros((32, 256), F32)
    for p in range(8):
        target = target + fine_decode(came_ref[p, 0:32, :]) * parts[:, p : p + 1]
    target = target / jnp.sum(parts, axis=1, keepdims=True) * (1.0 / (ROOT * PAIRS))
    hi, lo = split(target)
    row = lax.broadcasted_iota(jnp.int32, (160, 32), 0)
    col = lax.broadcasted_iota(jnp.int32, (160, 32), 1)
    keep = jnp.where((row // CROPS == col // GLOBAL) & (row % CROPS != col % GLOBAL), 1.0, 0.0).astype(BF16)
    student = [fine_decode(came_ref[p, 32:64, :])[:20] for p in range(8)]
    total = jnp.concatenate(student, axis=0) * (1.0 / WIDE) - (dot(keep, hi, NN) + dot(keep, lo, NN))
    x = feat_ref[...].astype(F32)
    norm = jnp.sqrt(jnp.sum(x * x, axis=1, keepdims=True) + 1e-06)
    unit = x / norm
    out_ref[...] = (total - unit * jnp.sum(unit * total, axis=1, keepdims=True)) / norm


def final_kernel(
    core_ref, came_ref, keep_ref, seen_ref, mate_ref, term_ref, term_mate_ref, weight_ref, scale_ref, inv_ref, out_ref
):
    first = core_ref[0] == 0
    rows = came_ref[0, 48:64, :].astype(F32)
    for p in range(1, 8):
        rows = rows + came_ref[p, 48:64, :].astype(F32)
    row_inv = lanes(1.0 / join_row(rows[8:])) * (1.0 / PAIRS)
    seen = seen_ref[...]
    mate = mate_ref[...]
    low_hi, low_lo = split(jnp.where(first, seen, mate) * row_inv[:, :512])
    high_hi, high_lo = split(jnp.where(first, mate, seen) * row_inv[:, 512:])
    for j in range(4):
        cols = slice(128 * j, 128 * j + 128)
        keep = keep_ref[cols, :]
        x = dot(low_hi, keep[:, :512], NT) + dot(low_lo, keep[:, :512], NT)
        x = x + (dot(high_hi, keep[:, 512:], NT) + dot(high_lo, keep[:, 512:], NT))
        x = term_ref[:, cols] + term_mate_ref[:, cols] - x * scale_ref[:, cols]
        w = weight_ref[:, cols].astype(F32)
        dots = jnp.sum(w * x, axis=0, keepdims=True) * inv_ref[:, cols]
        out_ref[:, cols] = x - w * dots


def columns(x):
    return jnp.concatenate([x, jnp.zeros((128 - x.shape[0], 256), F32)], axis=0).T


def exp_kernel(
    core_ref, own_ref, mate_ref, unit_ref, out_ref, sum_ref, all_ref, my_ref, my_scale_ref, my_inv_ref, hi_ref, lo_ref,
    scale_ref,
):
    step = pl.program_id(0)

    @pl.when(step == 0)
    def _():
        first = core_ref[0] == 0
        squares = jnp.zeros((8, 1024), F32)
        for p in range(16):
            block = []
            for ref in (own_ref, mate_ref):
                x = ref[2 * p].astype(F32)
                y = ref[2 * p + 1].astype(F32)
                top = jnp.concatenate([x[:8], x[8:]], axis=1)
                block.append(jnp.concatenate([top, jnp.concatenate([y[:8], y[8:]], axis=1)], axis=0))
            own, mate = block
            left = jnp.where(first, own, mate)
            right = jnp.where(first, mate, own)
            rows = slice(16 * p, 16 * p + 16)
            all_ref[rows, :512] = left.astype(BF16)
            all_ref[rows, 512:] = right.astype(BF16)
            my_ref[rows, :] = own.astype(BF16)
            both = jnp.concatenate([left, right], axis=1)
            both = both * both
            squares = squares + (both[:8] + both[8:])
        norm_sq = jnp.sum(squares, axis=0, keepdims=True) + 1e-06
        scale = 1.0 / (jnp.sqrt(norm_sq) * STUDENT_TEMP)
        scale_ref[...] = scale
        my_inv_ref[...] = 1.0 / jnp.where(first, norm_sq[:, :512], norm_sq[:, 512:])
        my_scale = jnp.where(first, scale[:, :512], scale[:, 512:])
        my_scale_ref[...] = my_scale
        for p in range(8):
            rows = slice(32 * p, 32 * p + 32)
            hi, lo = split(my_ref[rows, :].astype(F32) * my_scale)
            hi_ref[rows, :] = hi
            lo_ref[rows, :] = lo

    scale = scale_ref[...]
    power = scale * LOG2E
    sums = []
    for p in range(4):
        for half in range(2):
            raw = dot(unit_ref[2 * p + half], all_ref[...], NN)
            prob = jnp.exp2(raw * power)
            sums.append(jnp.sum(prob, axis=1, keepdims=True))
            out_ref[160 * p + 80 * half : 160 * p + 80 * half + 80, :] = (prob * scale).astype(BF16)
    sums = [jnp.concatenate(sums[2 * p : 2 * p + 2], axis=0) for p in range(4)]
    sums = jnp.concatenate(sums + [jnp.ones((160, 124), F32)], axis=1)
    sums = jnp.concatenate([sums, jnp.ones((96, 128), F32)], axis=0).T[:4]
    row = lax.broadcasted_iota(jnp.int32, (16, 256), 0)
    sum_ref[...] = jnp.where(row // 4 == step, jnp.concatenate([sums] * 4, axis=0), sum_ref[...])


def student_kernel(grad_ref, weight_ref, part_ref, out_ref):
    scale = columns(ROOT / part_ref[...])
    for p in range(8):
        x = dot(grad_ref[160 * p : 160 * p + 160, :], weight_ref[...], NT)
        x = root_code(x * scale[:160, p : p + 1]).astype(BF16)
        out_ref[2 * p, 0:80, :] = x[:80]
        out_ref[2 * p + 1, 0:80, :] = x[80:]


def seen_kernel(unit_ref, out_ref):
    row = lax.broadcasted_iota(jnp.int32, (16, 80), 0)
    col = lax.broadcasted_iota(jnp.int32, (16, 80), 1)
    keep = (col // CROPS == row // GLOBAL) & (col % CROPS != row % GLOBAL)
    keep = jnp.where(keep, 1.0, 0.0).astype(BF16)
    for j in range(4):
        block = [dot(keep, unit_ref[p], NN) for p in range(8 * j, 8 * j + 8)]
        out_ref[:, 128 * j : 128 * j + 128] = jnp.concatenate(block, axis=0).T


def term_kernel(core_ref, unit_ref, grad_ref, came_ref, own_ref, other_ref, total_ref):
    step = pl.program_id(0)
    first = core_ref[0] == 0
    exp_sum = sum_decode(came_ref[0, 32:48, :])
    for p in range(1, 8):
        exp_sum = exp_sum + sum_decode(came_ref[p, 32:48, :])
    exp_sum = jnp.where(step == 0, exp_sum[:8], exp_sum[8:]) * 16.0
    row = lax.broadcasted_iota(jnp.int32, (8, 256), 1)
    weight = jnp.where(row % CROPS < GLOBAL, (GLOBAL - 1) / PAIRS, GLOBAL / PAIRS)
    factor = columns(jnp.where(row < 160, weight / exp_sum, 0.0))
    for j in range(2):
        parts = []
        for p in range(4 * j, 4 * j + 4):
            unit = jnp.concatenate([unit_ref[2 * p], unit_ref[2 * p + 1]], axis=0).astype(F32)
            parts.append(unit * factor[:160, p : p + 1])
        hi, lo = split(jnp.concatenate(parts, axis=0))
        grad = grad_ref[640 * j : 640 * j + 640, :]
        x = dot(hi, grad, TN) + dot(lo, grad, TN)
        if j == 0:
            total_ref[...] = x + jnp.where(step == 0, 0.0, total_ref[...])
        else:
            total_ref[...] += x

    @pl.when(step == 1)
    def _():
        left = total_ref[:, :512]
        right = total_ref[:, 512:]
        own_ref[...] = jnp.where(first, left, right)
        other_ref[...] = jnp.where(first, right, left)


VMEM = pl.BlockSpec(memory_space=pltpu.VMEM)
SMEM = pl.BlockSpec(memory_space=pltpu.SMEM)


def call(kernel, shapes, flops, moved, *args, specs=None, room=32, **more):
    if specs is None:
        specs = [SMEM if x.ndim == 1 and x.dtype == jnp.int32 else VMEM for x in args]
    return pl.pallas_call(
        kernel,
        out_shape=shapes,
        in_specs=specs,
        cost_estimate=pl.CostEstimate(flops=flops, bytes_accessed=moved, transcendentals=0),
        compiler_params=pltpu.CompilerParams(vmem_limit_bytes=room * 1024 * 1024),
        **more,
    )(*args)


def shape(dims, dtype=F32):
    return pltpu.HBM(dims, dtype)


def hbm(x):
    return pltpu.with_memory_space_constraint(x, pltpu.HBM)


def shards(student_feat, prototypes, teacher_logits):
    core = lax.axis_index("core")
    core_arg = core.reshape(1)
    index = lax.axis_index(BATCH).reshape(1)
    place = jnp.stack([lax.axis_index(PLANE), lax.axis_index("proto"), core])
    whole = lambda *dims: pl.BlockSpec(dims, lambda i: (0,) * len(dims))

    send = call(
        pack_kernel,
        shape((32, 160, 256), BF16),
        10**7,
        5 * 10**6,
        teacher_logits,
        prototypes,
        student_feat,
        specs=[pl.BlockSpec((32, 8192), lambda i: (0, i)), pl.BlockSpec((8, 8192), lambda i: (0, i)), whole(160, 256)],
        out_specs=pl.BlockSpec((16, 160, 256), lambda i: (i, 0, 0)),
        scratch_shapes=[pltpu.VMEM((160, 256), BF16)],
        grid=(2,),
        room=56,
    )
    got = lax.all_to_all(send, BATCH, 0, 0, tiled=True)

    mate = lax.ppermute(got[:, 64:80], "core", SWAP)
    mass, pack = call(
        first_kernel,
        (shape((512, 1024)), shape((32, 8, 128))),
        10**7,
        3 * 10**6,
        got,
        specs=[whole(32, 64, 256)],
        out_specs=(VMEM, VMEM),
        grid=(1,),
    )
    got, mate, pack = lax.optimization_barrier((got, mate, pack))
    came = lax.all_to_all(pack, BATCH, 0, 0, tiled=True)
    row_sum = jnp.sum(came, axis=0)
    grad_prob, exp_part, weights, my_weights, my_scale, my_inv, unit_hi, unit_lo = call(
        exp_kernel,
        (
            shape((2560, 1024), BF16),
            shape((16, 256)),
            shape((256, 1024), BF16),
            shape((256, 512), BF16),
            shape((1, 512)),
            shape((1, 512)),
            shape((256, 512), BF16),
            shape((256, 512), BF16),
        ),
        2 * 10**9,
        9 * 10**6,
        core_arg,
        got,
        mate,
        got,
        specs=[
            SMEM,
            pl.BlockSpec((32, 16, 256), lambda i: (0, 4, 0)),
            whole(32, 16, 256),
            pl.BlockSpec((8, 80, 256), lambda i: (i, 1, 0)),
        ],
        out_specs=(
            pl.BlockSpec((640, 1024), lambda i: (i, 0)),
            whole(16, 256),
            whole(256, 1024),
            whole(256, 512),
            whole(1, 512),
            whole(1, 512),
            whole(256, 512),
            whole(256, 512),
        ),
        scratch_shapes=[pltpu.VMEM((1, 1024), F32)],
        grid=(4,),
    )
    unit_spec = pl.BlockSpec((16, 80, 256), lambda i: (i, 1, 0))

    grad_prob, row_sum = lax.optimization_barrier((grad_prob, row_sum))
    came_one = lax.all_to_all(jnp.broadcast_to(row_sum[None], (8, 8, 128)), "proto", 0, 0, tiled=True)
    student_pack = call(
        student_kernel,
        shape((32, 96, 256), BF16),
        2 * 10**9,
        7 * 10**6,
        hbm(grad_prob),
        hbm(weights),
        exp_part,
        specs=[
            pl.BlockSpec((1280, 1024), lambda i: (i, 0)),
            whole(256, 1024),
            pl.BlockSpec((8, 256), lambda i: (i, 0)),
        ],
        out_specs=pl.BlockSpec((16, 96, 256), lambda i: (i, 0, 0)),
        grid=(2,),
    )
    came_one, student_pack = lax.optimization_barrier((came_one, student_pack))

    pack = call(
        second_kernel,
        shape((32, 96, 256), BF16),
        10**7,
        2 * 10**6,
        came_one,
        exp_part,
        hbm(mass),
        hbm(student_pack),
        specs=[VMEM, VMEM, pl.BlockSpec(memory_space=pltpu.HBM), pl.BlockSpec(memory_space=pltpu.HBM)],
        out_specs=pl.BlockSpec((32, 16, 256), lambda i: (0, 5, 0)),
        scratch_shapes=[pltpu.VMEM((512, 1024), F32), pltpu.SemaphoreType.DMA((8,))],
        grid=(1,),
        input_output_aliases={3: 0},
    )
    came = lax.all_to_all(pack, BATCH, 0, 0, tiled=True)

    got, _ = lax.optimization_barrier((got, pack))
    seen = call(
        seen_kernel,
        shape((256, 512)),
        10**8,
        2 * 10**6,
        got,
        specs=[pl.BlockSpec((32, 80, 256), lambda i: (0, 1, 0))],
        out_specs=VMEM,
        grid=(1,),
    )
    seen_mate = lax.ppermute(seen, "core", SWAP)

    pack = call(
        home_kernel,
        shape((8, 48, 256), BF16),
        10**7,
        2 * 10**6,
        place,
        hbm(came),
        specs=[SMEM, whole(32, 96, 256)],
        out_specs=whole(8, 48, 256),
        grid=(1,),
    )
    came_two = lax.all_to_all(pack, "proto", 0, 0, tiled=True)

    keep, pack = call(
        third_kernel,
        (shape((512, 1024), BF16), shape((32, 40, 256), BF16)),
        10**9,
        4 * 10**6,
        came_two,
        came_one,
        mass,
        unit_hi,
        unit_lo,
        out_specs=(VMEM, VMEM),
    )
    came = lax.all_to_all(pack, BATCH, 0, 0, tiled=True)

    came_two, _ = lax.optimization_barrier((came_two, pack))
    term, other = call(
        term_kernel,
        (shape((256, 512)), shape((256, 512))),
        3 * 10**9,
        7 * 10**6,
        core_arg,
        got,
        hbm(grad_prob),
        came_two,
        specs=[SMEM, unit_spec, pl.BlockSpec((1280, 1024), lambda i: (i, 0)), VMEM],
        out_specs=(VMEM, VMEM),
        scratch_shapes=[pltpu.VMEM((256, 1024), F32)],
        grid=(2,),
    )
    term_mate = lax.ppermute(other, "core", SWAP)
    home_slice = call(slice_kernel, shape((24, 256)), 10**6, 10**5, place, came_two, out_specs=VMEM)

    pack = call(
        target_kernel,
        shape((8, 64, 256), BF16),
        10**7,
        10**6,
        index,
        came,
        home_slice,
        out_specs=VMEM,
        scratch_shapes=[pltpu.VMEM((128, 128), F32)],
    )
    came = lax.all_to_all(pack, "proto", 0, 0, tiled=True)

    grad = call(
        final_kernel,
        shape((256, 512)),
        10**9,
        4 * 10**6,
        core_arg,
        came,
        hbm(keep),
        hbm(seen),
        hbm(seen_mate),
        hbm(term),
        hbm(term_mate),
        hbm(my_weights),
        my_scale,
        my_inv,
        specs=[SMEM, VMEM, whole(512, 1024)] + [whole(256, 512)] * 5 + [VMEM, VMEM],
        out_specs=whole(256, 512),
        grid=(1,),
    )
    came, student_feat, _ = lax.optimization_barrier((came, student_feat, grad))
    grad = lax.all_to_all(grad.reshape(32, 8, 512), BATCH, 0, 0, tiled=True)
    grad_weight = grad.transpose(1, 0, 2).reshape(8, 16384)
    grad_feat = call(
        feat_kernel,
        shape((160, 256)),
        10**7,
        10**6,
        index,
        came,
        student_feat,
        out_specs=VMEM,
        scratch_shapes=[pltpu.VMEM((128, 128), F32)],
    )
    return (grad_feat, grad_weight)


def solution(mesh):
    split_mesh = Mesh(mesh.devices.reshape(4, 4, 2, 8), ("y", "x", "core", "proto"))
    return jax.shard_map(
        shards,
        mesh=split_mesh,
        in_specs=(P(BATCH, None), P(BATCH, "proto"), P(BATCH, "proto")),
        out_specs=(P(BATCH, None), P(BATCH, "proto")),
        check_vma=False,
    )
```

```python
import jax
import jax.numpy as jnp
from jax import lax
from jax.experimental import pallas as pl
from jax.experimental.pallas import tpu as pltpu
from jax.sharding import Mesh, PartitionSpec as P

CROPS = 10
GLOBAL = 2
STUDENT_TEMP = 0.1
TEACHER_TEMP = 0.04
PAIRS = float(GLOBAL * CROPS - GLOBAL)
F32 = jnp.float32
BF16 = jnp.bfloat16
PLANE = ("y", "x")
BATCH = ("y", "x", "core")
SWAP = ((0, 1), (1, 0))
SPAN = 250.0
LOW = 125.0
LOG2E = 1.4426950408889634
ROOT = 3276.8
WIDE = 16384.0
TINY = 1e-38


def encode_logits(x):
    mag = jnp.exp2(jnp.abs(x) * SPAN - LOW)
    return jnp.where(x < 0, -mag, mag).astype(BF16)


def decode_exp(code):
    v = code.astype(F32)
    mag = (jnp.log2(jnp.abs(v)) + LOW) * (LOG2E / (TEACHER_TEMP * SPAN))
    return jnp.exp2(jnp.where(v < 0, -mag, mag))


def root_code(x):
    y = x * x
    y = y * y
    return jnp.where(x < 0, -y, y)


def root_decode(code):
    v = code.astype(F32)
    y = lax.rsqrt(lax.rsqrt(jnp.abs(v) + TINY))
    return jnp.where(v < 0, -y, y)


def fine_code(x):
    y = x * x
    y = y * y
    y = y * y
    return jnp.where(x < 0, -y, y)


def fine_decode(code):
    v = code.astype(F32)
    y = jnp.sqrt(lax.rsqrt(lax.rsqrt(jnp.abs(v) + TINY)))
    return jnp.where(v < 0, -y, y)


def sum_code(x):
    y = x * (1.0 / 1024.0)
    y = y * y
    y = y * y
    return y * y


def sum_decode(code):
    return jnp.sqrt(lax.rsqrt(lax.rsqrt(code.astype(F32)))) * 1024.0


def split(x):
    hi = x.astype(BF16)
    return hi, (x - hi.astype(F32)).astype(BF16)


def dot(a, b, dims):
    return lax.dot_general(a, b, (dims, ((), ())), preferred_element_type=F32)


NN = ((1,), (0,))
NT = ((1,), (1,))
TN = ((0,), (0,))


def lanes(x8):
    return jnp.concatenate([x8[i : i + 1] for i in range(8)], axis=1)


def rows8(x):
    return jnp.concatenate([x[:, 128 * i : 128 * (i + 1)] for i in range(8)], axis=0)


def split_row(x8):
    hi = x8.astype(BF16).astype(F32)
    return jnp.concatenate([hi, x8 - hi], axis=1)


def join_row(x):
    return x[:, :128] + x[:, 128:]


def padded(x8):
    return jnp.concatenate([x8, jnp.zeros_like(x8)], axis=0).astype(BF16)


def sweep(mass_ref, row_inv, keep_ref=None):
    total = jnp.zeros((8, 1024), F32)
    for low in range(0, 512, 32):
        x = mass_ref[low : low + 32, :]
        y = x if row_inv is None else x * row_inv
        x = x * (1.0 / jnp.sum(y, axis=1, keepdims=True))
        if keep_ref is not None:
            keep_ref[low : low + 32, :] = x.astype(BF16)
        total = total + ((x[:8] + x[8:16]) + (x[16:24] + x[24:]))
    return jnp.sum(total, axis=0, keepdims=True)


def pack_kernel(teacher_ref, proto_ref, feat_ref, out_ref, unit_ref):
    @pl.when(pl.program_id(0) == 0)
    def _():
        x = feat_ref[...].astype(F32)
        unit = x / jnp.sqrt(jnp.sum(x * x, axis=1, keepdims=True) + 1e-06)
        unit_ref[...] = unit.astype(BF16)

    for p in range(16):
        cols = 512 * p
        out_ref[p, 0:32, :] = encode_logits(teacher_ref[:, cols : cols + 256]).astype(BF16)
        out_ref[p, 32:64, :] = encode_logits(teacher_ref[:, cols + 256 : cols + 512]).astype(BF16)
        w = proto_ref[:, cols : cols + 512].astype(F32)
        out_ref[p, 64:80, :] = jnp.concatenate([w[:, :256], w[:, 256:]], axis=0).astype(BF16)
        out_ref[p, 80:160, :] = unit_ref[80 * (p % 2) : 80 * (p % 2) + 80, :]


def fill(own_ref, mass_ref):
    for h in range(2):
        for j in range(4):
            cols = slice(512 * h + 128 * j, 512 * h + 128 * j + 128)
            for side in range(2):
                low = 32 * side + 16 * h
                block = own_ref[8 * j : 8 * j + 8, low : low + 16, :].reshape(128, 256)
                mass_ref[256 * side : 256 * side + 256, cols] = decode_exp(block).T


def first_kernel(own_ref, out_ref, mass_ref):
    fill(own_ref, mass_ref)
    part = rows8(sweep(mass_ref, None))
    out_ref[...] = jnp.broadcast_to(part[None], (32, 8, 128))


def second_kernel(came_ref, sum_ref, own_ref, pack_ref, out_ref, mass_ref):
    fill(own_ref, mass_ref)
    row_inv = lanes(1.0 / jnp.sum(came_ref[...], axis=0))
    part = rows8(sweep(mass_ref, row_inv) * row_inv)
    part = root_code(part * WIDE)
    part = jnp.concatenate([part[:, :64], part[:, 64:]], axis=0)
    row = jnp.concatenate([sum_code(sum_ref[...])[:, :192], part], axis=1).astype(BF16)
    out_ref[...] = jnp.broadcast_to(row[None], (32, 16, 256))


def home_kernel(place_ref, came_ref, out_ref):
    core = place_ref[2]
    pick = lax.broadcasted_iota(jnp.int32, (16, 256), 0) == place_ref[0]
    row_sum = jnp.zeros((16, 128), F32)
    parts = [[], []]
    exp_sum = jnp.zeros((16, 256), F32)
    for p in range(32):
        row_sum = row_sum + root_decode(came_ref[p, 80:96, 128:])
        exp_part = sum_decode(came_ref[p, 80:96, :])
        exp_sum = exp_sum + jnp.where(core == p % 2, exp_part, 0.0)
        parts[p % 2].append(jnp.sum(jnp.where(pick, exp_part, 0.0), axis=0, keepdims=True))
    code = []
    home_sum = []
    for half in range(2):
        x = jnp.concatenate(parts[half], axis=0)
        x = jnp.where(core == 0, x[:, :80], x[:, 80:160])
        home_sum.append(jnp.sum(x, axis=0, keepdims=True))
        x = jnp.concatenate([x, jnp.ones((16, 176), F32)], axis=1)
        x = columns(x * (1.0 / ROOT))[:80]
        scale = 1.0 / jnp.sum(x, axis=1, keepdims=True)
        for low in range(0, 80, 16):
            home = jnp.zeros((16, 256), F32)
            for p in range(16):
                part = root_decode(came_ref[2 * p + half, low : low + 16, :])
                home = home + part * x[low : low + 16, p : p + 1]
            code.append(fine_code(home * scale[low : low + 16]))
    code = jnp.concatenate(code, axis=0)
    home_sum = jnp.concatenate(home_sum + [jnp.ones((1, 96), F32)], axis=1)
    row_sum = jnp.concatenate([row_sum[:8, 64:], row_sum[8:, 64:]], axis=1)
    lane = lax.broadcasted_iota(jnp.int32, (16, 256), 1)
    exp_sum = jnp.where(lane < 160, exp_sum, 1.0)
    tail = [
        sum_code(home_sum * (1.0 / 16.0)),
        jnp.zeros((3, 256), F32),
        split_row(row_sum),
        sum_code(exp_sum * (1.0 / 16.0)),
    ]
    for z in range(8):
        out_ref[z] = jnp.concatenate([code[20 * z : 20 * z + 20]] + tail, axis=0).astype(BF16)


def slice_kernel(place_ref, came_ref, out_ref):
    parts = [sum_decode(came_ref[p, 16:32, :])[4:5] * 16.0 for p in range(8)]
    parts = pltpu.roll(jnp.concatenate(parts, axis=0), (256 - 20 * place_ref[1]) % 256, 1)
    parts = columns(parts)[:32]
    home = jnp.zeros((32, 256), F32)
    for p in range(8):
        home = home + fine_decode(came_ref[p, 0:32, :]) * parts[:, p : p + 1]
    row = lax.broadcasted_iota(jnp.int32, (32, 1), 0)
    weight = jnp.where(row % CROPS < GLOBAL, (GLOBAL - 1) / PAIRS, GLOBAL / PAIRS) * (WIDE / ROOT)
    out_ref[...] = fine_code(home * (weight / jnp.sum(parts, axis=1, keepdims=True)))[:24]


def third_kernel(came_ref, came_one_ref, mass_ref, hi_ref, lo_ref, keep_ref, out_ref):
    rows = jnp.zeros((16, 256), F32)
    for p in range(8):
        rows = rows + came_ref[p, 16:32, :].astype(F32)
    row_inv = lanes(WIDE / (join_row(rows[8:]) * jnp.sum(came_one_ref[...], axis=0)))
    part = sweep(mass_ref, row_inv, keep_ref)
    scale = ROOT / part
    tail = split_row(rows8(part))
    for j in range(4):
        both = []
        for h in range(2):
            cols = slice(512 * h + 128 * j, 512 * h + 128 * j + 128)
            keep = keep_ref[:, cols]
            x = jnp.dot(hi_ref[...], keep, preferred_element_type=F32)
            x = x + jnp.dot(lo_ref[...], keep, preferred_element_type=F32)
            both.append(root_code((x * scale[:, cols]).T))
        for i in range(8):
            rows = slice(16 * i, 16 * i + 16)
            out_ref[8 * j + i] = jnp.concatenate([both[0][rows], both[1][rows], tail], axis=0).astype(BF16)


def home_columns(rows, index, turn_ref):
    pick = lax.broadcasted_iota(jnp.int32, (8, 128), 0) - index // 8
    pad = jnp.zeros((128 - len(rows), 128), F32)
    both = []
    for h in range(2):
        picked = [jnp.sum(jnp.where(pick == 4 * h, row, 0.0), axis=0, keepdims=True) for row in rows]
        turn_ref[...] = jnp.concatenate(picked + [pad], axis=0).T
        both.append(turn_ref[pl.ds(pl.multiple_of(index % 8 * 16, 16), 16), :])
    return jnp.concatenate(both, axis=0)


def target_kernel(index_ref, came_ref, slice_ref, out_ref, turn_ref):
    rows = [join_row(came_ref[p].astype(F32)[32:]) for p in range(32)]
    row_sum = rows[0]
    for p in range(1, 32):
        row_sum = row_sum + rows[p]
    parts = home_columns(rows, index_ref[0], turn_ref) * (1.0 / ROOT)
    total = jnp.zeros((32, 256), F32)
    for p in range(32):
        total = total + root_decode(came_ref[p])[:32] * parts[:, p : p + 1]
    code = fine_code(total / jnp.sum(parts, axis=1, keepdims=True))
    code = jnp.concatenate([code, slice_ref[...], split_row(row_sum)], axis=0).astype(BF16)
    out_ref[...] = jnp.broadcast_to(code[None], (8, 64, 256))


def feat_kernel(index_ref, came_ref, feat_ref, out_ref, turn_ref):
    rows = [join_row(came_ref[p, 48:64, :].astype(F32)[8:]) for p in range(8)]
    parts = home_columns(rows, index_ref[0], turn_ref)
    target = jnp.zeros((32, 256), F32)
    for p in range(8):
        target = target + fine_decode(came_ref[p, 0:32, :]) * parts[:, p : p + 1]
    target = target / jnp.sum(parts, axis=1, keepdims=True) * (1.0 / (ROOT * PAIRS))
    hi, lo = split(target)
    row = lax.broadcasted_iota(jnp.int32, (160, 32), 0)
    col = lax.broadcasted_iota(jnp.int32, (160, 32), 1)
    keep = jnp.where((row // CROPS == col // GLOBAL) & (row % CROPS != col % GLOBAL), 1.0, 0.0).astype(BF16)
    student = [fine_decode(came_ref[p, 32:64, :])[:20] for p in range(8)]
    total = jnp.concatenate(student, axis=0) * (1.0 / WIDE) - (dot(keep, hi, NN) + dot(keep, lo, NN))
    x = feat_ref[...].astype(F32)
    norm = jnp.sqrt(jnp.sum(x * x, axis=1, keepdims=True) + 1e-06)
    unit = x / norm
    out_ref[...] = (total - unit * jnp.sum(unit * total, axis=1, keepdims=True)) / norm


def final_kernel(
    core_ref, came_ref, keep_ref, seen_ref, mate_ref, term_ref, weight_ref, scale_ref, inv_ref, out_ref
):
    first = core_ref[0] == 0
    rows = came_ref[0, 48:64, :].astype(F32)
    for p in range(1, 8):
        rows = rows + came_ref[p, 48:64, :].astype(F32)
    row_inv = lanes(1.0 / join_row(rows[8:])) * (1.0 / PAIRS)
    seen = seen_ref[...]
    mate = mate_ref[...]
    low_hi, low_lo = split(jnp.where(first, seen, mate) * row_inv[:, :512])
    high_hi, high_lo = split(jnp.where(first, mate, seen) * row_inv[:, 512:])
    for j in range(4):
        cols = slice(128 * j, 128 * j + 128)
        keep = keep_ref[cols, :]
        x = dot(low_hi, keep[:, :512], NT) + dot(low_lo, keep[:, :512], NT)
        x = x + (dot(high_hi, keep[:, 512:], NT) + dot(high_lo, keep[:, 512:], NT))
        x = term_ref[:, cols] - x * scale_ref[:, cols]
        w = weight_ref[:, cols].astype(F32)
        dots = jnp.sum(w * x, axis=0, keepdims=True) * inv_ref[:, cols]
        out_ref[:, cols] = x - w * dots


def columns(x):
    return jnp.concatenate([x, jnp.zeros((128 - x.shape[0], 256), F32)], axis=0).T


def exp_kernel(
    core_ref, own_ref, mate_ref, unit_ref, out_ref, sum_ref, all_ref, my_ref, my_scale_ref, my_inv_ref, hi_ref, lo_ref,
    scale_ref,
):
    step = pl.program_id(0)

    @pl.when(step == 0)
    def _():
        first = core_ref[0] == 0
        squares = jnp.zeros((8, 1024), F32)
        for p in range(16):
            block = []
            for ref in (own_ref, mate_ref):
                x = ref[2 * p].astype(F32)
                y = ref[2 * p + 1].astype(F32)
                top = jnp.concatenate([x[:8], x[8:]], axis=1)
                block.append(jnp.concatenate([top, jnp.concatenate([y[:8], y[8:]], axis=1)], axis=0))
            own, mate = block
            left = jnp.where(first, own, mate)
            right = jnp.where(first, mate, own)
            rows = slice(16 * p, 16 * p + 16)
            all_ref[rows, :512] = left.astype(BF16)
            all_ref[rows, 512:] = right.astype(BF16)
            my_ref[rows, :] = own.astype(BF16)
            both = jnp.concatenate([left, right], axis=1)
            both = both * both
            squares = squares + (both[:8] + both[8:])
        norm_sq = jnp.sum(squares, axis=0, keepdims=True) + 1e-06
        scale = 1.0 / (jnp.sqrt(norm_sq) * STUDENT_TEMP)
        scale_ref[...] = scale
        my_inv_ref[...] = 1.0 / jnp.where(first, norm_sq[:, :512], norm_sq[:, 512:])
        my_scale = jnp.where(first, scale[:, :512], scale[:, 512:])
        my_scale_ref[...] = my_scale
        for p in range(8):
            rows = slice(32 * p, 32 * p + 32)
            hi, lo = split(my_ref[rows, :].astype(F32) * my_scale)
            hi_ref[rows, :] = hi
            lo_ref[rows, :] = lo

    scale = scale_ref[...]
    power = scale * LOG2E
    sums = []
    for p in range(4):
        for half in range(2):
            raw = dot(unit_ref[2 * p + half], all_ref[...], NN)
            prob = jnp.exp2(raw * power)
            sums.append(jnp.sum(prob, axis=1, keepdims=True))
            out_ref[160 * p + 80 * half : 160 * p + 80 * half + 80, :] = (prob * scale).astype(BF16)
    sums = [jnp.concatenate(sums[2 * p : 2 * p + 2], axis=0) for p in range(4)]
    sums = jnp.concatenate(sums + [jnp.ones((160, 124), F32)], axis=1)
    sums = jnp.concatenate([sums, jnp.ones((96, 128), F32)], axis=0).T[:4]
    row = lax.broadcasted_iota(jnp.int32, (16, 256), 0)
    sum_ref[...] = jnp.where(row // 4 == step, jnp.concatenate([sums] * 4, axis=0), sum_ref[...])


def student_kernel(grad_ref, weight_ref, part_ref, out_ref):
    scale = columns(ROOT / part_ref[...])
    for p in range(8):
        x = dot(grad_ref[160 * p : 160 * p + 160, :], weight_ref[...], NT)
        x = root_code(x * scale[:160, p : p + 1]).astype(BF16)
        out_ref[2 * p, 0:80, :] = x[:80]
        out_ref[2 * p + 1, 0:80, :] = x[80:]


def seen_kernel(unit_ref, out_ref):
    row = lax.broadcasted_iota(jnp.int32, (16, 80), 0)
    col = lax.broadcasted_iota(jnp.int32, (16, 80), 1)
    keep = (col // CROPS == row // GLOBAL) & (col % CROPS != row % GLOBAL)
    keep = jnp.where(keep, 1.0, 0.0).astype(BF16)
    for j in range(4):
        block = [dot(keep, unit_ref[p], NN) for p in range(8 * j, 8 * j + 8)]
        out_ref[:, 128 * j : 128 * j + 128] = jnp.concatenate(block, axis=0).T


def term_kernel(core_ref, unit_ref, grad_ref, came_ref, own_ref, other_ref, total_ref):
    step = pl.program_id(0)
    first = core_ref[0] == 0
    exp_sum = sum_decode(came_ref[0, 32:48, :])
    for p in range(1, 8):
        exp_sum = exp_sum + sum_decode(came_ref[p, 32:48, :])
    exp_sum = jnp.where(step == 0, exp_sum[:8], exp_sum[8:]) * 16.0
    row = lax.broadcasted_iota(jnp.int32, (8, 256), 1)
    weight = jnp.where(row % CROPS < GLOBAL, (GLOBAL - 1) / PAIRS, GLOBAL / PAIRS)
    factor = columns(jnp.where(row < 160, weight / exp_sum, 0.0))
    for j in range(2):
        parts = []
        for p in range(4 * j, 4 * j + 4):
            unit = jnp.concatenate([unit_ref[2 * p], unit_ref[2 * p + 1]], axis=0).astype(F32)
            parts.append(unit * factor[:160, p : p + 1])
        hi, lo = split(jnp.concatenate(parts, axis=0))
        grad = grad_ref[640 * j : 640 * j + 640, :]
        x = dot(hi, grad, TN) + dot(lo, grad, TN)
        if j == 0:
            total_ref[...] = x + jnp.where(step == 0, 0.0, total_ref[...])
        else:
            total_ref[...] += x

    @pl.when(step == 1)
    def _():
        left = total_ref[:, :512]
        right = total_ref[:, 512:]
        own_ref[...] = jnp.where(first, left, right)
        other_ref[...] = jnp.where(first, right, left)


VMEM = pl.BlockSpec(memory_space=pltpu.VMEM)
SMEM = pl.BlockSpec(memory_space=pltpu.SMEM)


def call(kernel, shapes, flops, moved, *args, specs=None, room=32, **more):
    if specs is None:
        specs = [SMEM if x.ndim == 1 and x.dtype == jnp.int32 else VMEM for x in args]
    return pl.pallas_call(
        kernel,
        out_shape=shapes,
        in_specs=specs,
        cost_estimate=pl.CostEstimate(flops=flops, bytes_accessed=moved, transcendentals=0),
        compiler_params=pltpu.CompilerParams(vmem_limit_bytes=room * 1024 * 1024),
        **more,
    )(*args)


def shape(dims, dtype=F32):
    return pltpu.HBM(dims, dtype)


def hbm(x):
    return pltpu.with_memory_space_constraint(x, pltpu.HBM)


def shards(student_feat, prototypes, teacher_logits):
    core = lax.axis_index("core")
    core_arg = core.reshape(1)
    index = lax.axis_index(BATCH).reshape(1)
    place = jnp.stack([lax.axis_index(PLANE), lax.axis_index("proto"), core])
    whole = lambda *dims: pl.BlockSpec(dims, lambda i: (0,) * len(dims))

    send = call(
        pack_kernel,
        shape((32, 160, 256), BF16),
        10**7,
        5 * 10**6,
        teacher_logits,
        prototypes,
        student_feat,
        specs=[pl.BlockSpec((32, 8192), lambda i: (0, i)), pl.BlockSpec((8, 8192), lambda i: (0, i)), whole(160, 256)],
        out_specs=pl.BlockSpec((16, 160, 256), lambda i: (i, 0, 0)),
        scratch_shapes=[pltpu.VMEM((160, 256), BF16)],
        grid=(2,),
        room=56,
    )
    got = lax.all_to_all(send, BATCH, 0, 0, tiled=True)

    mate = lax.ppermute(got[:, 64:80], "core", SWAP)
    teacher_spec = whole(32, 64, 256)
    pack = call(
        first_kernel,
        shape((32, 8, 128)),
        10**7,
        10**6,
        got,
        specs=[teacher_spec],
        out_specs=VMEM,
        scratch_shapes=[pltpu.VMEM((512, 1024), F32)],
        grid=(1,),
    )
    got, mate, pack = lax.optimization_barrier((got, mate, pack))
    came = lax.all_to_all(pack, BATCH, 0, 0, tiled=True)
    row_sum = jnp.sum(came, axis=0)
    grad_prob, exp_part, weights, my_weights, my_scale, my_inv, unit_hi, unit_lo = call(
        exp_kernel,
        (
            shape((2560, 1024), BF16),
            shape((16, 256)),
            shape((256, 1024), BF16),
            shape((256, 512), BF16),
            shape((1, 512)),
            shape((1, 512)),
            shape((256, 512), BF16),
            shape((256, 512), BF16),
        ),
        2 * 10**9,
        9 * 10**6,
        core_arg,
        got,
        mate,
        got,
        specs=[
            SMEM,
            pl.BlockSpec((32, 16, 256), lambda i: (0, 4, 0)),
            whole(32, 16, 256),
            pl.BlockSpec((8, 80, 256), lambda i: (i, 1, 0)),
        ],
        out_specs=(
            pl.BlockSpec((640, 1024), lambda i: (i, 0)),
            whole(16, 256),
            whole(256, 1024),
            whole(256, 512),
            whole(1, 512),
            whole(1, 512),
            whole(256, 512),
            whole(256, 512),
        ),
        scratch_shapes=[pltpu.VMEM((1, 1024), F32)],
        grid=(4,),
    )
    unit_spec = pl.BlockSpec((16, 80, 256), lambda i: (i, 1, 0))

    grad_prob, row_sum = lax.optimization_barrier((grad_prob, row_sum))
    came_one = lax.all_to_all(jnp.broadcast_to(row_sum[None], (8, 8, 128)), "proto", 0, 0, tiled=True)
    student_pack = call(
        student_kernel,
        shape((32, 96, 256), BF16),
        2 * 10**9,
        7 * 10**6,
        hbm(grad_prob),
        hbm(weights),
        exp_part,
        specs=[
            pl.BlockSpec((1280, 1024), lambda i: (i, 0)),
            whole(256, 1024),
            pl.BlockSpec((8, 256), lambda i: (i, 0)),
        ],
        out_specs=pl.BlockSpec((16, 96, 256), lambda i: (i, 0, 0)),
        grid=(2,),
    )
    came_one, student_pack = lax.optimization_barrier((came_one, student_pack))

    pack = call(
        second_kernel,
        shape((32, 96, 256), BF16),
        10**7,
        2 * 10**6,
        came_one,
        exp_part,
        got,
        hbm(student_pack),
        specs=[VMEM, VMEM, teacher_spec, pl.BlockSpec(memory_space=pltpu.HBM)],
        out_specs=pl.BlockSpec((32, 16, 256), lambda i: (0, 5, 0)),
        scratch_shapes=[pltpu.VMEM((512, 1024), F32)],
        grid=(1,),
        input_output_aliases={3: 0},
    )
    came = lax.all_to_all(pack, BATCH, 0, 0, tiled=True)

    got, _ = lax.optimization_barrier((got, pack))
    seen = call(
        seen_kernel,
        shape((256, 512)),
        10**8,
        2 * 10**6,
        got,
        specs=[pl.BlockSpec((32, 80, 256), lambda i: (0, 1, 0))],
        out_specs=VMEM,
        grid=(1,),
    )
    seen_mate = lax.ppermute(seen, "core", SWAP)
    mass = call(fill, shape((512, 1024)), 10**7, 3 * 10**6, got, specs=[teacher_spec], out_specs=VMEM, grid=(1,))

    came, mass = lax.optimization_barrier((came, mass))
    pack = call(
        home_kernel,
        shape((8, 48, 256), BF16),
        10**7,
        2 * 10**6,
        place,
        hbm(came),
        specs=[SMEM, whole(32, 96, 256)],
        out_specs=whole(8, 48, 256),
        grid=(1,),
    )
    came_two = lax.all_to_all(pack, "proto", 0, 0, tiled=True)

    keep, pack = call(
        third_kernel,
        (shape((512, 1024), BF16), shape((32, 40, 256), BF16)),
        10**9,
        4 * 10**6,
        came_two,
        came_one,
        mass,
        unit_hi,
        unit_lo,
        out_specs=(VMEM, VMEM),
    )
    came = lax.all_to_all(pack, BATCH, 0, 0, tiled=True)

    came_two, _ = lax.optimization_barrier((came_two, pack))
    term, other = call(
        term_kernel,
        (shape((256, 512)), shape((256, 512))),
        3 * 10**9,
        7 * 10**6,
        core_arg,
        got,
        hbm(grad_prob),
        came_two,
        specs=[SMEM, unit_spec, pl.BlockSpec((1280, 1024), lambda i: (i, 0)), VMEM],
        out_specs=(VMEM, VMEM),
        scratch_shapes=[pltpu.VMEM((256, 1024), F32)],
        grid=(2,),
    )
    term = term + lax.ppermute(other, "core", SWAP)
    home_slice = call(slice_kernel, shape((24, 256)), 10**6, 10**5, place, came_two, out_specs=VMEM)

    pack = call(
        target_kernel,
        shape((8, 64, 256), BF16),
        10**7,
        10**6,
        index,
        came,
        home_slice,
        out_specs=VMEM,
        scratch_shapes=[pltpu.VMEM((128, 128), F32)],
    )
    came = lax.all_to_all(pack, "proto", 0, 0, tiled=True)

    grad = call(
        final_kernel,
        shape((256, 512)),
        10**9,
        4 * 10**6,
        core_arg,
        came,
        hbm(keep),
        hbm(seen),
        hbm(seen_mate),
        hbm(term),
        hbm(my_weights),
        my_scale,
        my_inv,
        specs=[SMEM, VMEM, whole(512, 1024)] + [whole(256, 512)] * 4 + [VMEM, VMEM],
        out_specs=whole(256, 512),
        grid=(1,),
    )
    came, student_feat, _ = lax.optimization_barrier((came, student_feat, grad))
    grad = lax.all_to_all(grad.reshape(32, 8, 512), BATCH, 0, 0, tiled=True)
    grad_weight = grad.transpose(1, 0, 2).reshape(8, 16384)
    grad_feat = call(
        feat_kernel,
        shape((160, 256)),
        10**7,
        10**6,
        index,
        came,
        student_feat,
        out_specs=VMEM,
        scratch_shapes=[pltpu.VMEM((128, 128), F32)],
    )
    return (grad_feat, grad_weight)


def solution(mesh):
    split_mesh = Mesh(mesh.devices.reshape(4, 4, 2, 8), ("y", "x", "core", "proto"))
    return jax.shard_map(
        shards,
        mesh=split_mesh,
        in_specs=(P(BATCH, None), P(BATCH, "proto"), P(BATCH, "proto")),
        out_specs=(P(BATCH, None), P(BATCH, "proto")),
        check_vma=False,
    )
```

```python
import jax
import jax.numpy as jnp
from jax import lax
from jax.experimental import pallas as pl
from jax.experimental.pallas import tpu as pltpu
from jax.sharding import Mesh, PartitionSpec as P

CROPS = 10
GLOBAL = 2
STUDENT_TEMP = 0.1
TEACHER_TEMP = 0.04
PAIRS = float(GLOBAL * CROPS - GLOBAL)
F32 = jnp.float32
BF16 = jnp.bfloat16
PLANE = ("y", "x")
BATCH = ("y", "x", "core")
SWAP = ((0, 1), (1, 0))
SPAN = 250.0
LOW = 125.0
LOG2E = 1.4426950408889634
ROOT = 3276.8
WIDE = 16384.0
TINY = 1e-38


def encode_logits(x):
    mag = jnp.exp2(jnp.abs(x) * SPAN - LOW)
    return jnp.where(x < 0, -mag, mag).astype(BF16)


def decode_exp(code):
    v = code.astype(F32)
    mag = (jnp.log2(jnp.abs(v)) + LOW) * (LOG2E / (TEACHER_TEMP * SPAN))
    return jnp.exp2(jnp.where(v < 0, -mag, mag))


def root_code(x):
    y = x * x
    y = y * y
    return jnp.where(x < 0, -y, y)


def root_decode(code):
    v = code.astype(F32)
    y = lax.rsqrt(lax.rsqrt(jnp.abs(v) + TINY))
    return jnp.where(v < 0, -y, y)


def fine_code(x):
    y = x * x
    y = y * y
    y = y * y
    return jnp.where(x < 0, -y, y)


def fine_decode(code):
    v = code.astype(F32)
    y = jnp.sqrt(lax.rsqrt(lax.rsqrt(jnp.abs(v) + TINY)))
    return jnp.where(v < 0, -y, y)


def sum_code(x):
    y = x * (1.0 / 1024.0)
    y = y * y
    y = y * y
    return y * y


def sum_decode(code):
    return jnp.sqrt(lax.rsqrt(lax.rsqrt(code.astype(F32)))) * 1024.0


def split(x):
    hi = x.astype(BF16)
    return hi, (x - hi.astype(F32)).astype(BF16)


def dot(a, b, dims):
    return lax.dot_general(a, b, (dims, ((), ())), preferred_element_type=F32)


NN = ((1,), (0,))
NT = ((1,), (1,))
TN = ((0,), (0,))


def lanes(x8):
    return jnp.concatenate([x8[i : i + 1] for i in range(8)], axis=1)


def rows8(x):
    return jnp.concatenate([x[:, 128 * i : 128 * (i + 1)] for i in range(8)], axis=0)


def split_row(x8):
    hi = x8.astype(BF16).astype(F32)
    return jnp.concatenate([hi, x8 - hi], axis=1)


def join_row(x):
    return x[:, :128] + x[:, 128:]


def padded(x8):
    return jnp.concatenate([x8, jnp.zeros_like(x8)], axis=0).astype(BF16)


def sweep(mass_ref, row_inv, keep_ref=None):
    total = jnp.zeros((8, 1024), F32)
    for low in range(0, 512, 32):
        x = mass_ref[low : low + 32, :]
        y = x if row_inv is None else x * row_inv
        x = x * (1.0 / jnp.sum(y, axis=1, keepdims=True))
        if keep_ref is not None:
            keep_ref[low : low + 32, :] = x.astype(BF16)
        total = total + ((x[:8] + x[8:16]) + (x[16:24] + x[24:]))
    return jnp.sum(total, axis=0, keepdims=True)


def pack_kernel(teacher_ref, proto_ref, feat_ref, out_ref, unit_ref):
    @pl.when(pl.program_id(0) == 0)
    def _():
        x = feat_ref[...].astype(F32)
        unit = x / jnp.sqrt(jnp.sum(x * x, axis=1, keepdims=True) + 1e-06)
        unit_ref[...] = unit.astype(BF16)

    for p in range(16):
        cols = 512 * p
        out_ref[p, 0:32, :] = encode_logits(teacher_ref[:, cols : cols + 256]).astype(BF16)
        out_ref[p, 32:64, :] = encode_logits(teacher_ref[:, cols + 256 : cols + 512]).astype(BF16)
        w = proto_ref[:, cols : cols + 512].astype(F32)
        out_ref[p, 64:80, :] = jnp.concatenate([w[:, :256], w[:, 256:]], axis=0).astype(BF16)
        out_ref[p, 80:160, :] = unit_ref[80 * (p % 2) : 80 * (p % 2) + 80, :]


def fill(own_ref, mass_ref):
    for h in range(2):
        for j in range(4):
            cols = slice(512 * h + 128 * j, 512 * h + 128 * j + 128)
            for side in range(2):
                low = 32 * side + 16 * h
                block = own_ref[8 * j : 8 * j + 8, low : low + 16, :].reshape(128, 256)
                mass_ref[256 * side : 256 * side + 256, cols] = decode_exp(block).T


def first_kernel(own_ref, out_ref, mass_ref):
    fill(own_ref, mass_ref)
    part = rows8(sweep(mass_ref, None))
    out_ref[...] = jnp.broadcast_to(part[None], (32, 8, 128))


def second_kernel(came_ref, sum_ref, own_ref, pack_ref, out_ref, mass_ref):
    fill(own_ref, mass_ref)
    row_inv = lanes(1.0 / jnp.sum(came_ref[...], axis=0))
    part = rows8(sweep(mass_ref, row_inv) * row_inv)
    part = root_code(part * WIDE)
    part = jnp.concatenate([part[:, :64], part[:, 64:]], axis=0)
    row = jnp.concatenate([sum_code(sum_ref[...])[:, :192], part], axis=1).astype(BF16)
    out_ref[...] = jnp.broadcast_to(row[None], (32, 16, 256))


def home_kernel(place_ref, came_hbm, out_ref, sum_ref, part_ref, sems):
    copies = [pltpu.make_async_copy(came_hbm.at[:, pl.ds(80, 16), :], sum_ref, sems.at[0])]
    for i in range(4):
        some = pl.ds(8 * i, 8)
        copies.append(
            pltpu.make_async_copy(came_hbm.at[some, pl.ds(0, 80), :], part_ref.at[some], sems.at[i + 1])
        )
    for copy in copies:
        copy.start()
    copies[0].wait()
    core = place_ref[2]
    pick = lax.broadcasted_iota(jnp.int32, (16, 256), 0) == place_ref[0]
    row_sum = jnp.zeros((16, 128), F32)
    parts = [[], []]
    exp_sum = jnp.zeros((16, 256), F32)
    for p in range(32):
        row_sum = row_sum + root_decode(sum_ref[p, :, 128:])
        exp_part = sum_decode(sum_ref[p])
        exp_sum = exp_sum + jnp.where(core == p % 2, exp_part, 0.0)
        parts[p % 2].append(jnp.sum(jnp.where(pick, exp_part, 0.0), axis=0, keepdims=True))
    home_sum = []
    factors = []
    for half in range(2):
        x = jnp.concatenate(parts[half], axis=0)
        x = jnp.where(core == 0, x[:, :80], x[:, 80:160])
        home_sum.append(jnp.sum(x, axis=0, keepdims=True))
        x = jnp.concatenate([x, jnp.ones((16, 176), F32)], axis=1)
        factors.append(columns(x * (1.0 / ROOT))[:80])
    home = [jnp.zeros((16, 256), F32)] * 10
    for i in range(4):
        copies[i + 1].wait()
        for p in range(8 * i, 8 * i + 8):
            half = p % 2
            for j in range(5):
                rows = slice(16 * j, 16 * j + 16)
                part = root_decode(part_ref[p, rows, :]) * factors[half][rows, p // 2 : p // 2 + 1]
                home[5 * half + j] = home[5 * half + j] + part
    home = jnp.concatenate(home, axis=0)
    scale = [1.0 / jnp.sum(x, axis=1, keepdims=True) for x in factors]
    code = [fine_code(home * jnp.concatenate(scale, axis=0))]
    code = jnp.concatenate(code, axis=0)
    home_sum = jnp.concatenate(home_sum + [jnp.ones((1, 96), F32)], axis=1)
    row_sum = jnp.concatenate([row_sum[:8, 64:], row_sum[8:, 64:]], axis=1)
    lane = lax.broadcasted_iota(jnp.int32, (16, 256), 1)
    exp_sum = jnp.where(lane < 160, exp_sum, 1.0)
    tail = [
        sum_code(home_sum * (1.0 / 16.0)),
        jnp.zeros((3, 256), F32),
        split_row(row_sum),
        sum_code(exp_sum * (1.0 / 16.0)),
    ]
    for z in range(8):
        out_ref[z] = jnp.concatenate([code[20 * z : 20 * z + 20]] + tail, axis=0).astype(BF16)


def slice_kernel(place_ref, came_ref, out_ref):
    parts = [sum_decode(came_ref[p, 16:32, :])[4:5] * 16.0 for p in range(8)]
    parts = pltpu.roll(jnp.concatenate(parts, axis=0), (256 - 20 * place_ref[1]) % 256, 1)
    parts = columns(parts)[:32]
    home = jnp.zeros((32, 256), F32)
    for p in range(8):
        home = home + fine_decode(came_ref[p, 0:32, :]) * parts[:, p : p + 1]
    row = lax.broadcasted_iota(jnp.int32, (32, 1), 0)
    weight = jnp.where(row % CROPS < GLOBAL, (GLOBAL - 1) / PAIRS, GLOBAL / PAIRS) * (WIDE / ROOT)
    out_ref[...] = fine_code(home * (weight / jnp.sum(parts, axis=1, keepdims=True)))[:24]


def third_kernel(came_ref, came_one_ref, mass_ref, hi_ref, lo_ref, keep_ref, out_ref):
    rows = jnp.zeros((16, 256), F32)
    for p in range(8):
        rows = rows + came_ref[p, 16:32, :].astype(F32)
    row_inv = lanes(WIDE / (join_row(rows[8:]) * jnp.sum(came_one_ref[...], axis=0)))
    part = sweep(mass_ref, row_inv, keep_ref)
    scale = ROOT / part
    tail = split_row(rows8(part))
    for j in range(4):
        both = []
        for h in range(2):
            cols = slice(512 * h + 128 * j, 512 * h + 128 * j + 128)
            keep = keep_ref[:, cols]
            x = jnp.dot(hi_ref[...], keep, preferred_element_type=F32)
            x = x + jnp.dot(lo_ref[...], keep, preferred_element_type=F32)
            both.append(root_code((x * scale[:, cols]).T))
        for i in range(8):
            rows = slice(16 * i, 16 * i + 16)
            out_ref[8 * j + i] = jnp.concatenate([both[0][rows], both[1][rows], tail], axis=0).astype(BF16)


def home_columns(rows, index, turn_ref):
    pick = lax.broadcasted_iota(jnp.int32, (8, 128), 0) - index // 8
    pad = jnp.zeros((128 - len(rows), 128), F32)
    both = []
    for h in range(2):
        picked = [jnp.sum(jnp.where(pick == 4 * h, row, 0.0), axis=0, keepdims=True) for row in rows]
        turn_ref[...] = jnp.concatenate(picked + [pad], axis=0).T
        both.append(turn_ref[pl.ds(pl.multiple_of(index % 8 * 16, 16), 16), :])
    return jnp.concatenate(both, axis=0)


def target_kernel(index_ref, came_ref, slice_ref, out_ref, turn_ref):
    rows = [join_row(came_ref[p].astype(F32)[32:]) for p in range(32)]
    row_sum = rows[0]
    for p in range(1, 32):
        row_sum = row_sum + rows[p]
    parts = home_columns(rows, index_ref[0], turn_ref) * (1.0 / ROOT)
    total = jnp.zeros((32, 256), F32)
    for p in range(32):
        total = total + root_decode(came_ref[p])[:32] * parts[:, p : p + 1]
    code = fine_code(total / jnp.sum(parts, axis=1, keepdims=True))
    code = jnp.concatenate([code, slice_ref[...], split_row(row_sum)], axis=0).astype(BF16)
    out_ref[...] = jnp.broadcast_to(code[None], (8, 64, 256))


def feat_kernel(index_ref, came_ref, feat_ref, out_ref, turn_ref):
    rows = [join_row(came_ref[p, 48:64, :].astype(F32)[8:]) for p in range(8)]
    parts = home_columns(rows, index_ref[0], turn_ref)
    target = jnp.zeros((32, 256), F32)
    for p in range(8):
        target = target + fine_decode(came_ref[p, 0:32, :]) * parts[:, p : p + 1]
    target = target / jnp.sum(parts, axis=1, keepdims=True) * (1.0 / (ROOT * PAIRS))
    hi, lo = split(target)
    row = lax.broadcasted_iota(jnp.int32, (160, 32), 0)
    col = lax.broadcasted_iota(jnp.int32, (160, 32), 1)
    keep = jnp.where((row // CROPS == col // GLOBAL) & (row % CROPS != col % GLOBAL), 1.0, 0.0).astype(BF16)
    student = [fine_decode(came_ref[p, 32:64, :])[:20] for p in range(8)]
    total = jnp.concatenate(student, axis=0) * (1.0 / WIDE) - (dot(keep, hi, NN) + dot(keep, lo, NN))
    x = feat_ref[...].astype(F32)
    norm = jnp.sqrt(jnp.sum(x * x, axis=1, keepdims=True) + 1e-06)
    unit = x / norm
    out_ref[...] = (total - unit * jnp.sum(unit * total, axis=1, keepdims=True)) / norm


def final_kernel(
    core_ref, came_ref, keep_ref, seen_ref, mate_ref, term_ref, weight_ref, scale_ref, inv_ref, out_ref
):
    first = core_ref[0] == 0
    rows = came_ref[0, 48:64, :].astype(F32)
    for p in range(1, 8):
        rows = rows + came_ref[p, 48:64, :].astype(F32)
    row_inv = lanes(1.0 / join_row(rows[8:])) * (1.0 / PAIRS)
    seen = seen_ref[...]
    mate = mate_ref[...]
    low_hi, low_lo = split(jnp.where(first, seen, mate) * row_inv[:, :512])
    high_hi, high_lo = split(jnp.where(first, mate, seen) * row_inv[:, 512:])
    for j in range(4):
        cols = slice(128 * j, 128 * j + 128)
        keep = keep_ref[cols, :]
        x = dot(low_hi, keep[:, :512], NT) + dot(low_lo, keep[:, :512], NT)
        x = x + (dot(high_hi, keep[:, 512:], NT) + dot(high_lo, keep[:, 512:], NT))
        x = term_ref[:, cols] - x * scale_ref[:, cols]
        w = weight_ref[:, cols].astype(F32)
        dots = jnp.sum(w * x, axis=0, keepdims=True) * inv_ref[:, cols]
        out_ref[:, cols] = x - w * dots


def columns(x):
    return jnp.concatenate([x, jnp.zeros((128 - x.shape[0], 256), F32)], axis=0).T


def exp_kernel(
    core_ref, own_ref, mate_ref, unit_ref, out_ref, sum_ref, all_ref, my_ref, my_scale_ref, my_inv_ref, hi_ref, lo_ref,
    scale_ref,
):
    step = pl.program_id(0)

    @pl.when(step == 0)
    def _():
        first = core_ref[0] == 0
        squares = jnp.zeros((8, 1024), F32)
        for p in range(16):
            block = []
            for ref in (own_ref, mate_ref):
                x = ref[2 * p].astype(F32)
                y = ref[2 * p + 1].astype(F32)
                top = jnp.concatenate([x[:8], x[8:]], axis=1)
                block.append(jnp.concatenate([top, jnp.concatenate([y[:8], y[8:]], axis=1)], axis=0))
            own, mate = block
            left = jnp.where(first, own, mate)
            right = jnp.where(first, mate, own)
            rows = slice(16 * p, 16 * p + 16)
            all_ref[rows, :512] = left.astype(BF16)
            all_ref[rows, 512:] = right.astype(BF16)
            my_ref[rows, :] = own.astype(BF16)
            both = jnp.concatenate([left, right], axis=1)
            both = both * both
            squares = squares + (both[:8] + both[8:])
        norm_sq = jnp.sum(squares, axis=0, keepdims=True) + 1e-06
        scale = 1.0 / (jnp.sqrt(norm_sq) * STUDENT_TEMP)
        scale_ref[...] = scale
        my_inv_ref[...] = 1.0 / jnp.where(first, norm_sq[:, :512], norm_sq[:, 512:])
        my_scale = jnp.where(first, scale[:, :512], scale[:, 512:])
        my_scale_ref[...] = my_scale
        for p in range(8):
            rows = slice(32 * p, 32 * p + 32)
            hi, lo = split(my_ref[rows, :].astype(F32) * my_scale)
            hi_ref[rows, :] = hi
            lo_ref[rows, :] = lo

    scale = scale_ref[...]
    power = scale * LOG2E
    sums = []
    for p in range(4):
        for half in range(2):
            raw = dot(unit_ref[2 * p + half], all_ref[...], NN)
            prob = jnp.exp2(raw * power)
            sums.append(jnp.sum(prob, axis=1, keepdims=True))
            out_ref[160 * p + 80 * half : 160 * p + 80 * half + 80, :] = (prob * scale).astype(BF16)
    sums = [jnp.concatenate(sums[2 * p : 2 * p + 2], axis=0) for p in range(4)]
    sums = jnp.concatenate(sums + [jnp.ones((160, 124), F32)], axis=1)
    sums = jnp.concatenate([sums, jnp.ones((96, 128), F32)], axis=0).T[:4]
    row = lax.broadcasted_iota(jnp.int32, (16, 256), 0)
    sum_ref[...] = jnp.where(row // 4 == step, jnp.concatenate([sums] * 4, axis=0), sum_ref[...])


def student_kernel(grad_ref, weight_ref, part_ref, out_ref):
    scale = columns(ROOT / part_ref[...])
    for p in range(8):
        x = dot(grad_ref[160 * p : 160 * p + 160, :], weight_ref[...], NT)
        x = root_code(x * scale[:160, p : p + 1]).astype(BF16)
        out_ref[2 * p, 0:80, :] = x[:80]
        out_ref[2 * p + 1, 0:80, :] = x[80:]


def seen_kernel(unit_ref, out_ref):
    row = lax.broadcasted_iota(jnp.int32, (16, 80), 0)
    col = lax.broadcasted_iota(jnp.int32, (16, 80), 1)
    keep = (col // CROPS == row // GLOBAL) & (col % CROPS != row % GLOBAL)
    keep = jnp.where(keep, 1.0, 0.0).astype(BF16)
    for j in range(4):
        block = [dot(keep, unit_ref[p], NN) for p in range(8 * j, 8 * j + 8)]
        out_ref[:, 128 * j : 128 * j + 128] = jnp.concatenate(block, axis=0).T


def term_kernel(core_ref, unit_ref, grad_ref, came_ref, own_ref, other_ref, total_ref):
    step = pl.program_id(0)
    first = core_ref[0] == 0
    exp_sum = sum_decode(came_ref[0, 32:48, :])
    for p in range(1, 8):
        exp_sum = exp_sum + sum_decode(came_ref[p, 32:48, :])
    exp_sum = jnp.where(step == 0, exp_sum[:8], exp_sum[8:]) * 16.0
    row = lax.broadcasted_iota(jnp.int32, (8, 256), 1)
    weight = jnp.where(row % CROPS < GLOBAL, (GLOBAL - 1) / PAIRS, GLOBAL / PAIRS)
    factor = columns(jnp.where(row < 160, weight / exp_sum, 0.0))
    for j in range(2):
        parts = []
        for p in range(4 * j, 4 * j + 4):
            unit = jnp.concatenate([unit_ref[2 * p], unit_ref[2 * p + 1]], axis=0).astype(F32)
            parts.append(unit * factor[:160, p : p + 1])
        hi, lo = split(jnp.concatenate(parts, axis=0))
        grad = grad_ref[640 * j : 640 * j + 640, :]
        x = dot(hi, grad, TN) + dot(lo, grad, TN)
        if j == 0:
            total_ref[...] = x + jnp.where(step == 0, 0.0, total_ref[...])
        else:
            total_ref[...] += x

    @pl.when(step == 1)
    def _():
        left = total_ref[:, :512]
        right = total_ref[:, 512:]
        own_ref[...] = jnp.where(first, left, right)
        other_ref[...] = jnp.where(first, right, left)


VMEM = pl.BlockSpec(memory_space=pltpu.VMEM)
SMEM = pl.BlockSpec(memory_space=pltpu.SMEM)


def call(kernel, shapes, flops, moved, *args, specs=None, room=32, **more):
    if specs is None:
        specs = [SMEM if x.ndim == 1 and x.dtype == jnp.int32 else VMEM for x in args]
    return pl.pallas_call(
        kernel,
        out_shape=shapes,
        in_specs=specs,
        cost_estimate=pl.CostEstimate(flops=flops, bytes_accessed=moved, transcendentals=0),
        compiler_params=pltpu.CompilerParams(vmem_limit_bytes=room * 1024 * 1024),
        **more,
    )(*args)


def shape(dims, dtype=F32):
    return pltpu.HBM(dims, dtype)


def hbm(x):
    return pltpu.with_memory_space_constraint(x, pltpu.HBM)


def shards(student_feat, prototypes, teacher_logits):
    core = lax.axis_index("core")
    core_arg = core.reshape(1)
    index = lax.axis_index(BATCH).reshape(1)
    place = jnp.stack([lax.axis_index(PLANE), lax.axis_index("proto"), core])
    whole = lambda *dims: pl.BlockSpec(dims, lambda i: (0,) * len(dims))

    send = call(
        pack_kernel,
        shape((32, 160, 256), BF16),
        10**7,
        5 * 10**6,
        teacher_logits,
        prototypes,
        student_feat,
        specs=[pl.BlockSpec((32, 8192), lambda i: (0, i)), pl.BlockSpec((8, 8192), lambda i: (0, i)), whole(160, 256)],
        out_specs=pl.BlockSpec((16, 160, 256), lambda i: (i, 0, 0)),
        scratch_shapes=[pltpu.VMEM((160, 256), BF16)],
        grid=(2,),
        room=56,
    )
    got = lax.all_to_all(send, BATCH, 0, 0, tiled=True)

    mate = lax.ppermute(got[:, 64:80], "core", SWAP)
    teacher_spec = whole(32, 64, 256)
    pack = call(
        first_kernel,
        shape((32, 8, 128)),
        10**7,
        10**6,
        got,
        specs=[teacher_spec],
        out_specs=VMEM,
        scratch_shapes=[pltpu.VMEM((512, 1024), F32)],
        grid=(1,),
    )
    got, mate, pack = lax.optimization_barrier((got, mate, pack))
    came = lax.all_to_all(pack, BATCH, 0, 0, tiled=True)
    row_sum = jnp.sum(came, axis=0)
    grad_prob, exp_part, weights, my_weights, my_scale, my_inv, unit_hi, unit_lo = call(
        exp_kernel,
        (
            shape((2560, 1024), BF16),
            shape((16, 256)),
            shape((256, 1024), BF16),
            shape((256, 512), BF16),
            shape((1, 512)),
            shape((1, 512)),
            shape((256, 512), BF16),
            shape((256, 512), BF16),
        ),
        2 * 10**9,
        9 * 10**6,
        core_arg,
        got,
        mate,
        got,
        specs=[
            SMEM,
            pl.BlockSpec((32, 16, 256), lambda i: (0, 4, 0)),
            whole(32, 16, 256),
            pl.BlockSpec((8, 80, 256), lambda i: (i, 1, 0)),
        ],
        out_specs=(
            pl.BlockSpec((640, 1024), lambda i: (i, 0)),
            whole(16, 256),
            whole(256, 1024),
            whole(256, 512),
            whole(1, 512),
            whole(1, 512),
            whole(256, 512),
            whole(256, 512),
        ),
        scratch_shapes=[pltpu.VMEM((1, 1024), F32)],
        grid=(4,),
    )
    unit_spec = pl.BlockSpec((16, 80, 256), lambda i: (i, 1, 0))

    grad_prob, row_sum = lax.optimization_barrier((grad_prob, row_sum))
    came_one = lax.all_to_all(jnp.broadcast_to(row_sum[None], (8, 8, 128)), "proto", 0, 0, tiled=True)
    student_pack = call(
        student_kernel,
        shape((32, 96, 256), BF16),
        2 * 10**9,
        7 * 10**6,
        hbm(grad_prob),
        hbm(weights),
        exp_part,
        specs=[
            pl.BlockSpec((1280, 1024), lambda i: (i, 0)),
            whole(256, 1024),
            pl.BlockSpec((8, 256), lambda i: (i, 0)),
        ],
        out_specs=pl.BlockSpec((16, 96, 256), lambda i: (i, 0, 0)),
        grid=(2,),
    )
    came_one, student_pack = lax.optimization_barrier((came_one, student_pack))

    pack = call(
        second_kernel,
        shape((32, 96, 256), BF16),
        10**7,
        2 * 10**6,
        came_one,
        exp_part,
        got,
        hbm(student_pack),
        specs=[VMEM, VMEM, teacher_spec, pl.BlockSpec(memory_space=pltpu.HBM)],
        out_specs=pl.BlockSpec((32, 16, 256), lambda i: (0, 5, 0)),
        scratch_shapes=[pltpu.VMEM((512, 1024), F32)],
        grid=(1,),
        input_output_aliases={3: 0},
    )
    came = lax.all_to_all(pack, BATCH, 0, 0, tiled=True)

    got, _ = lax.optimization_barrier((got, pack))
    seen = call(
        seen_kernel,
        shape((256, 512)),
        10**8,
        2 * 10**6,
        got,
        specs=[pl.BlockSpec((32, 80, 256), lambda i: (0, 1, 0))],
        out_specs=VMEM,
        grid=(1,),
    )
    seen_mate = lax.ppermute(seen, "core", SWAP)
    mass = call(fill, shape((512, 1024)), 10**7, 3 * 10**6, got, specs=[teacher_spec], out_specs=VMEM, grid=(1,))

    came, mass = lax.optimization_barrier((came, mass))
    pack = call(
        home_kernel,
        shape((8, 48, 256), BF16),
        10**7,
        2 * 10**6,
        place,
        hbm(came),
        specs=[SMEM, pl.BlockSpec(memory_space=pltpu.HBM)],
        out_specs=whole(8, 48, 256),
        scratch_shapes=[
            pltpu.VMEM((32, 16, 256), BF16),
            pltpu.VMEM((32, 80, 256), BF16),
            pltpu.SemaphoreType.DMA((5,)),
        ],
        grid=(1,),
    )
    came_two = lax.all_to_all(pack, "proto", 0, 0, tiled=True)

    keep, pack = call(
        third_kernel,
        (shape((512, 1024), BF16), shape((32, 40, 256), BF16)),
        10**9,
        4 * 10**6,
        came_two,
        came_one,
        mass,
        unit_hi,
        unit_lo,
        out_specs=(VMEM, VMEM),
    )
    came = lax.all_to_all(pack, BATCH, 0, 0, tiled=True)

    came_two, _ = lax.optimization_barrier((came_two, pack))
    term, other = call(
        term_kernel,
        (shape((256, 512)), shape((256, 512))),
        3 * 10**9,
        7 * 10**6,
        core_arg,
        got,
        hbm(grad_prob),
        came_two,
        specs=[SMEM, unit_spec, pl.BlockSpec((1280, 1024), lambda i: (i, 0)), VMEM],
        out_specs=(VMEM, VMEM),
        scratch_shapes=[pltpu.VMEM((256, 1024), F32)],
        grid=(2,),
    )
    term = term + lax.ppermute(other, "core", SWAP)
    home_slice = call(slice_kernel, shape((24, 256)), 10**6, 10**5, place, came_two, out_specs=VMEM)

    pack = call(
        target_kernel,
        shape((8, 64, 256), BF16),
        10**7,
        10**6,
        index,
        came,
        home_slice,
        out_specs=VMEM,
        scratch_shapes=[pltpu.VMEM((128, 128), F32)],
    )
    came = lax.all_to_all(pack, "proto", 0, 0, tiled=True)

    grad = call(
        final_kernel,
        shape((256, 512)),
        10**9,
        4 * 10**6,
        core_arg,
        came,
        hbm(keep),
        hbm(seen),
        hbm(seen_mate),
        hbm(term),
        hbm(my_weights),
        my_scale,
        my_inv,
        specs=[SMEM, VMEM, whole(512, 1024)] + [whole(256, 512)] * 4 + [VMEM, VMEM],
        out_specs=whole(256, 512),
        grid=(1,),
    )
    came, student_feat, _ = lax.optimization_barrier((came, student_feat, grad))
    grad = lax.all_to_all(grad.reshape(32, 8, 512), BATCH, 0, 0, tiled=True)
    grad_weight = grad.transpose(1, 0, 2).reshape(8, 16384)
    grad_feat = call(
        feat_kernel,
        shape((160, 256)),
        10**7,
        10**6,
        index,
        came,
        student_feat,
        out_specs=VMEM,
        scratch_shapes=[pltpu.VMEM((128, 128), F32)],
    )
    return (grad_feat, grad_weight)


def solution(mesh):
    split_mesh = Mesh(mesh.devices.reshape(4, 4, 2, 8), ("y", "x", "core", "proto"))
    return jax.shard_map(
        shards,
        mesh=split_mesh,
        in_specs=(P(BATCH, None), P(BATCH, "proto"), P(BATCH, "proto")),
        out_specs=(P(BATCH, None), P(BATCH, "proto")),
        check_vma=False,
    )
```
